32 devices in a mesh: dp: 8 (over z, y), map: 4 (over x, core).
Axes of the slice: x: 2, y: 2, z: 4, core: 2. Of those that a mesh axis runs over, the one named last changes fastest.
Arguments:
- embeddings: bfloat16 [32768, 256], P('dp'), may hold values from -96 to 96
- winners: int32 [32768], P('dp'), may hold values from 0 to 65535, as said below
- codebook: float32 [256, 256, 256], P('dp', 'map'), may hold values from -6 to 6
Outputs:
- updated: float32 [256, 256, 256], P('dp', 'map')
- updated_copy: bfloat16 [256, 256, 256], P('dp', 'map')
The draws below stay inside these ranges and needn't reach their ends.
Inputs may be any that keep to these rules, and one draw needn't show every extreme that they name: `winners`: the winning node of each row, numbered c * 256 + r for map column c and map row r; within the rows of one index of dp (aligned blocks of 4096 rows), at most 256 rows win a node of any one tile of 256 / 8 map columns by 256 / 4 map rows (tile of columns c // (256 / 8) and rows r // (256 / 4)), and in every block some tile has exactly 256.
All inputs are finite; a program needn't handle non-finite values.
Results may differ from the reference program's by a relative error of at most 0.0075.
Values may be sent and summed in bfloat16 or wider, within the bound.
A program may use at most 64 MiB of HBM per device.

```python
import jax
import jax.numpy as jnp
from jax import lax

E = 256
MR = 256
MC = 256
ROWS_DEV = 4096
REACH = 16
ROWS = 32768
CAP = 256
N_DP = 8
N_MAP = 4


def draw_winners(key, part):
    groups = N_DP * N_MAP
    cols_tile = MC // N_DP
    rows_tile = MR // N_MAP

    def one_block(block_key):
        keys = jax.random.split(block_key, 5)
        full = jax.random.randint(keys[0], (), 0, groups).astype(jnp.int32)
        others = (jax.random.permutation(keys[1], (groups - 1) * CAP)[:ROWS_DEV - CAP] // CAP).astype(jnp.int32)
        others = others + (others >= full).astype(jnp.int32)
        labels = jnp.concatenate([jnp.zeros((CAP,), jnp.int32) + full, others])
        labels = jax.random.permutation(keys[2], labels).astype(jnp.int32)
        band_index = labels // N_DP
        column_block = labels - band_index * N_DP
        column = column_block * cols_tile + jax.random.randint(keys[3], (ROWS_DEV,), 0, cols_tile).astype(jnp.int32)
        row_value = band_index * rows_tile + jax.random.randint(keys[4], (ROWS_DEV,), 0, rows_tile).astype(jnp.int32)
        return (column * MR + row_value).astype(jnp.int32)
    block_keys = jax.random.split(jax.random.fold_in(key, 7), N_DP)
    return jax.vmap(one_block)(block_keys).reshape(-1).astype(jnp.int32)


def levels(key, extent, cuts, least, top_value):
    loudness, own = 1.0, jax.random.fold_in(key, 6)
    for axis_at, blocks in cuts:
        draws = jnp.exp(jax.random.uniform(jax.random.fold_in(own, axis_at), (blocks,), jnp.float32, least / len(cuts), top_value / len(cuts)))
        loudness = loudness * jnp.repeat(draws, extent[axis_at] // blocks).reshape([-1 if axis == axis_at else 1 for axis in range(len(extent))])
    return loudness


def centred(stream_key, shape, width, bound, cuts=(), kind=jnp.bfloat16):
    gain = levels(stream_key, shape, cuts, -0.22, 0.18) if cuts else 1.0
    values = jax.random.normal(stream_key, shape, jnp.float32) * width * gain
    return jnp.minimum(jnp.maximum(values, -bound), bound).astype(kind)


def setup_inputs(seed: int = 0) -> dict:
    arg_keys = jax.random.split(jax.random.key(seed), 4)
    return {
        "embeddings": centred(arg_keys[0], (ROWS, E), 16.0, 96.0, ((0, 8),)),
        "winners": draw_winners(jax.random.fold_in(arg_keys[3], 71), 0),
        "codebook": centred(arg_keys[2], (MC, MR, E), 1.0, 6.0, ((0, 8), (1, 4)), jnp.float32),
    }


def kernel(total, sigma, reach):
    place = jnp.arange(total, dtype=jnp.float32)
    gap = place[:, None] - place[None, :]
    apart = gap / sigma
    return jnp.where(jnp.abs(gap) <= reach, jnp.exp(-0.5 * apart * apart) / sigma, 0.0).astype(jnp.float32)


def reference(embeddings, winners, codebook):
    highest = lax.Precision.HIGHEST
    sigma = float(REACH) / 2.0
    raw = jax.ops.segment_sum(embeddings.astype(jnp.float32), winners, num_segments=MR * MC).reshape(MC, MR, E)
    counts = jax.ops.segment_sum(jnp.ones(winners.shape, jnp.float32), winners, num_segments=MR * MC).reshape(MC, MR)
    g_col = kernel(MC, sigma, REACH)
    g_row = kernel(MR, sigma, REACH)
    num = jnp.einsum("ac,cre->are", g_col, raw, precision=highest)
    num = jnp.einsum("br,are->abe", g_row, num, precision=highest)
    den = jnp.dot(g_col, counts, precision=highest)
    den = jnp.dot(den, g_row.T, precision=highest)
    updated = 0.1 * codebook + 0.9 * (num + codebook) / (den[:, :, None] + 1.0)
    return updated, updated.astype(jnp.bfloat16)
```

```python
import functools

import jax
import jax.numpy as jnp
from jax import lax
from jax.experimental import pallas as pl
from jax.experimental.pallas import tpu as pltpu
from jax.sharding import PartitionSpec as P

REACH = 16
SIGMA = float(REACH) / 2.0
PARTS = 2
MESH = pl.DeviceIdType.MESH
NT = (((1,), (1,)), ((), ()))


def iota(shape, dim):
    return lax.broadcasted_iota(jnp.int32, shape, dim)


def over(values, size):
    if size & (size - 1) == 0:
        return lax.shift_right_logical(values, jnp.int32(size.bit_length() - 1))
    return values // size


def weight(gap):
    apart = gap / SIGMA
    return jnp.where(jnp.abs(gap) <= REACH, jnp.exp(-0.5 * apart * apart) / SIGMA, 0.0)


def exchange_kernel(
    dims, emb_ref, win_ref, ext_ref, den_ref,
    rank, tags, x_out, x_in, k_out, k_in, cw, rm, mix, own, h_out, h_in, d_out, d_in, d_own, t1, m_in, dm_in,
    x_ss, x_rs, k_ss, k_rs, h_ss, h_rs, d_ss, d_rs, m_ss, m_rs, dm_ss, dm_rs,
):
    n_dp, n_map, cap, cols, band, rows, width = dims
    part = width // PARTS
    slots = n_dp * cap
    edge = REACH * band
    me = lax.axis_index("dp")
    mm = lax.axis_index("map")
    left, right = lax.rem(me + n_dp - 1, n_dp), lax.rem(me + 1, n_dp)
    up, down = lax.rem(mm + n_map - 1, n_map), lax.rem(mm + 1, n_map)

    barrier = pltpu.get_barrier_semaphore()
    for k in range(1, n_dp):
        pl.semaphore_signal(
            barrier, inc=1, device_id=(lax.rem(me + k, n_dp), mm), device_id_type=MESH
        )
    for other in (up, down):
        pl.semaphore_signal(barrier, inc=1, device_id=(me, other), device_id_type=MESH)

    win = win_ref[...]
    column = over(win, band * n_map)
    row_of = win - column * (band * n_map) - mm * band
    target = over(column, cols)
    local = column - target * cols
    inside = (row_of >= 0) & (row_of < band)
    target = jnp.where(inside, target, -1)
    which = iota((16, rows), 0)
    tags[...] = jnp.where(
        which == 0,
        local.astype(jnp.float32),
        jnp.where(which == 1, row_of.astype(jnp.float32), jnp.where(which == 2, 1.0, 0.0)),
    ).astype(jnp.bfloat16)
    step = 256
    upper = jnp.where(iota((step, step), 0) <= iota((step, step), 1), 1.0, 0.0).astype(jnp.bfloat16)
    hits = jnp.where(target == iota((n_dp, rows), 0), 1.0, 0.0)
    carry = jnp.zeros((n_dp, 1), jnp.float32)
    for j in range(rows // step):
        hit = hits[:, j * step : (j + 1) * step]
        count = jnp.dot(hit.astype(jnp.bfloat16), upper, preferred_element_type=jnp.float32) + carry
        carry = count[:, step - 1 : step]
        rank[:, j * step : (j + 1) * step] = jnp.where(hit > 0.0, count - 1.0, -1.0).astype(jnp.int32)

    pl.semaphore_wait(barrier, n_dp + 1)

    def pick(to):
        chosen = jnp.where(rank[pl.ds(to, 1), :] == iota((cap, rows), 0), 1.0, 0.0).astype(jnp.bfloat16)
        packed = jnp.dot(chosen, emb_ref[...], preferred_element_type=jnp.float32).astype(jnp.bfloat16)
        keys = lax.dot_general(tags[...], chosen, NT, preferred_element_type=jnp.float32)
        return packed, keys.astype(jnp.bfloat16)

    def x_copy(h, to, slot):
        return pltpu.make_async_remote_copy(
            src_ref=x_out.at[h, to],
            dst_ref=x_in.at[h, pl.ds(pl.multiple_of(slot * cap, cap), cap), :],
            send_sem=x_ss.at[h, to],
            recv_sem=x_rs.at[h, slot],
            device_id=(to, mm),
            device_id_type=MESH,
        )

    def k_copy(to, slot):
        return pltpu.make_async_remote_copy(
            src_ref=k_out.at[to],
            dst_ref=k_in.at[slot],
            send_sem=k_ss.at[to],
            recv_sem=k_rs.at[slot],
            device_id=(to, mm),
            device_id_type=MESH,
        )

    def partner(k):
        half = (k + 1) // 2
        return lax.rem(me + n_dp // 2 + half * (1 - 2 * (k % 2)), n_dp)

    def send(k, none):
        to = partner(k)
        packed, keys = pick(to)
        k_out[to] = keys
        for h in range(PARTS):
            x_out[h, to] = packed[:, h * part : (h + 1) * part]
        k_copy(to, me).start()
        x_copy(0, to, me).start()
        return none

    lax.fori_loop(0, n_dp - 1, send, 0)
    for h in range(1, PARTS):
        def send_later(k, none, h=h):
            x_copy(h, partner(k), me).start()
            return none

        lax.fori_loop(0, n_dp - 1, send_later, 0)
    packed, keys = pick(me)
    k_in[me] = keys
    for h in range(PARTS):
        x_in[h, pl.ds(pl.multiple_of(me * cap, cap), cap), :] = packed[:, h * part : (h + 1) * part]

    def take_keys(k, none):
        k_copy(partner(k), partner(k)).wait_recv()
        return none

    lax.fori_loop(0, n_dp - 1, take_keys, 0)

    span = cols + 2 * REACH
    for s in range(n_dp):
        key = k_in[s].astype(jnp.float32)
        gap = (iota((span, cap), 0) - REACH).astype(jnp.float32) - key[0:1, :]
        cw[:, s * cap : (s + 1) * cap] = weight(gap) * key[2:3, :]
        rm[:, s * cap : (s + 1) * cap] = jnp.where(
            iota((band, cap), 0).astype(jnp.float32) == key[1:2, :], 1.0, 0.0
        ).astype(jnp.bfloat16)

    def fill(a, none):
        line = jnp.broadcast_to(cw[pl.ds(a, 1), :], (band, slots)).astype(jnp.bfloat16)
        mix[pl.ds(pl.multiple_of(a * band, band), band), :] = line * rm[...]
        return none

    lax.fori_loop(0, span, fill, 0)
    den = lax.dot_general(
        cw[...].astype(jnp.bfloat16), rm[...], NT, preferred_element_type=jnp.float32
    )
    d_out[0] = den[:REACH]
    d_out[1] = den[REACH + cols :]
    d_own[...] = den[REACH : REACH + cols]

    def h_copy(h, side):
        return pltpu.make_async_remote_copy(
            src_ref=h_out.at[h, side],
            dst_ref=h_in.at[h, 1 - side],
            send_sem=h_ss.at[h, side],
            recv_sem=h_rs.at[h, 1 - side],
            device_id=((left, right)[side], mm),
            device_id_type=MESH,
        )

    def d_copy(side):
        return pltpu.make_async_remote_copy(
            src_ref=d_out.at[side],
            dst_ref=d_in.at[1 - side],
            send_sem=d_ss.at[side],
            recv_sem=d_rs.at[1 - side],
            device_id=((left, right)[side], mm),
            device_id_type=MESH,
        )

    def m_copy(h, side):
        start = 0 if side == 0 else band - REACH
        return pltpu.make_async_remote_copy(
            src_ref=t1.at[h, :, pl.ds(start, REACH), :],
            dst_ref=m_in.at[h, 1 - side],
            send_sem=m_ss.at[h, side],
            recv_sem=m_rs.at[h, 1 - side],
            device_id=(me, (up, down)[side]),
            device_id_type=MESH,
        )

    def dm_copy(side):
        return pltpu.make_async_remote_copy(
            src_ref=d_own,
            dst_ref=dm_in.at[1 - side],
            send_sem=dm_ss.at[side],
            recv_sem=dm_rs.at[1 - side],
            device_id=(me, (up, down)[side]),
            device_id_type=MESH,
        )

    has_dp = (me > 0, me < n_dp - 1)
    has_map = (mm > 0, mm < n_map - 1)

    for side in range(2):
        @pl.when(has_dp[side])
        def _(side=side):
            d_copy(side).start()

    for h in range(PARTS):
        def take(k, none, h=h):
            x_copy(h, partner(k), partner(k)).wait_recv()
            return none

        lax.fori_loop(0, n_dp - 1, take, 0)
        for side in range(2):
            base = 0 if side == 0 else (REACH + cols) * band
            h_out[h, side] = jnp.dot(
                mix[base : base + edge, :], x_in[h], preferred_element_type=jnp.float32
            ).astype(jnp.bfloat16)

            @pl.when(has_dp[side])
            def _(side=side, h=h):
                h_copy(h, side).start()

        def keep(g, none, h=h):
            at = pl.multiple_of(g * edge, edge)
            own[h, pl.ds(at, edge), :] = jnp.dot(
                mix[pl.ds(pl.multiple_of(edge + at, edge), edge), :],
                x_in[h],
                preferred_element_type=jnp.float32,
            )
            return none

        lax.fori_loop(0, cols // REACH, keep, 0)

    for side in range(2):
        base = 0 if side == 0 else cols - REACH

        @pl.when(has_dp[side])
        def _(side=side, base=base):
            d_copy(1 - side).wait_recv()
            d_own[pl.ds(base, REACH), :] += d_in[side]

    for side in range(2):
        @pl.when(has_map[side])
        def _(side=side):
            dm_copy(side).start()

    for h in range(PARTS):
        for side in range(2):
            base = 0 if side == 0 else (cols - REACH) * band

            @pl.when(has_dp[side])
            def _(side=side, base=base, h=h):
                h_copy(h, 1 - side).wait_recv()
                own[h, pl.ds(base, edge), :] += h_in[h, side].astype(jnp.float32)

        t1[h] = own[h].astype(jnp.bfloat16).reshape(cols, band, part)
        for side in range(2):
            @pl.when(has_map[side])
            def _(side=side, h=h):
                m_copy(h, side).start()

        ext_ref[:, REACH : REACH + band, h * part : (h + 1) * part] = t1[h]
    den_ref[1] = d_own[...]

    for side in range(2):
        base = 0 if side == 0 else REACH + band

        @pl.when(has_map[side])
        def _(side=side, base=base):
            dm_copy(1 - side).wait_recv()
            den_ref[2 * side] = dm_in[side]
            for h in range(PARTS):
                m_copy(h, 1 - side).wait_recv()
                ext_ref[:, base : base + REACH, h * part : (h + 1) * part] = m_in[h, side]

        @pl.when(jnp.logical_not(has_map[side]))
        def _(side=side, base=base):
            den_ref[2 * side] = jnp.zeros((cols, band), jnp.float32)
            ext_ref[:, base : base + REACH, :] = jnp.zeros((cols, REACH, width), jnp.bfloat16)

    def sent(k, none):
        k_copy(partner(k), me).wait_send()
        for h in range(PARTS):
            x_copy(h, partner(k), me).wait_send()
        return none

    lax.fori_loop(0, n_dp - 1, sent, 0)
    for side in range(2):
        @pl.when(has_dp[side])
        def _(side=side):
            d_copy(side).wait_send()
            for h in range(PARTS):
                h_copy(h, side).wait_send()

        @pl.when(has_map[side])
        def _(side=side):
            dm_copy(side).wait_send()
            for h in range(PARTS):
                m_copy(h, side).wait_send()


def finish_kernel(ext_ref, den_ref, book_ref, new_ref, copy_ref):
    count, band, width = book_ref.shape
    reach_band = ext_ref.shape[1]
    gap = iota((band, reach_band), 0) + REACH - iota((band, reach_band), 1)
    smooth = weight(gap.astype(jnp.float32)).astype(jnp.bfloat16)
    den = jnp.zeros((band, count), jnp.float32)
    apart = (iota((band, band), 0) - iota((band, band), 1)).astype(jnp.float32)
    for p in range(3):
        taps = weight(apart + float((1 - p) * band)).astype(jnp.bfloat16).astype(jnp.float32)
        den += lax.dot_general(
            taps, den_ref[p], NT, precision=lax.Precision.HIGHEST, preferred_element_type=jnp.float32
        )
    scale = 0.9 / (den + 1.0)
    for i in range(count):
        num = jnp.dot(smooth, ext_ref[i], preferred_element_type=jnp.float32)
        book = book_ref[i]
        new = 0.1 * book + (num + book) * scale[:, i : i + 1]
        new_ref[i] = new
        copy_ref[i] = new.astype(jnp.bfloat16)


def on_device(embeddings, winners, codebook):
    cols, band, width = codebook.shape
    n_dp = lax.axis_size("dp")
    n_map = lax.axis_size("map")
    rows = embeddings.shape[0]
    cap = max(2, 2 * rows // (n_dp * n_map))
    slots = n_dp * cap
    part = width // PARTS
    span = cols + 2 * REACH
    edge = REACH * band
    bf16, f32 = jnp.bfloat16, jnp.float32
    vmem = pl.BlockSpec(memory_space=pltpu.VMEM)
    dma = pltpu.SemaphoreType.DMA
    ext, den = pl.pallas_call(
        functools.partial(exchange_kernel, (n_dp, n_map, cap, cols, band, rows, width)),
        out_shape=(
            jax.ShapeDtypeStruct((cols, band + 2 * REACH, width), bf16),
            jax.ShapeDtypeStruct((3, cols, band), f32),
        ),
        in_specs=[vmem, vmem],
        out_specs=(vmem, vmem),
        scratch_shapes=[
            pltpu.VMEM((n_dp, rows), jnp.int32),
            pltpu.VMEM((16, rows), bf16),
            pltpu.VMEM((PARTS, n_dp, cap, part), bf16),
            pltpu.VMEM((PARTS, slots, part), bf16),
            pltpu.VMEM((n_dp, 16, cap), bf16),
            pltpu.VMEM((n_dp, 16, cap), bf16),
            pltpu.VMEM((span, slots), f32),
            pltpu.VMEM((band, slots), bf16),
            pltpu.VMEM((span * band, slots), bf16),
            pltpu.VMEM((PARTS, cols * band, part), f32),
            pltpu.VMEM((PARTS, 2, edge, part), bf16),
            pltpu.VMEM((PARTS, 2, edge, part), bf16),
            pltpu.VMEM((2, REACH, band), f32),
            pltpu.VMEM((2, REACH, band), f32),
            pltpu.VMEM((cols, band), f32),
            pltpu.VMEM((PARTS, cols, band, part), bf16),
            pltpu.VMEM((PARTS, 2, cols, REACH, part), bf16),
            pltpu.VMEM((2, cols, band), f32),
            dma((PARTS, n_dp)), dma((PARTS, n_dp)), dma((n_dp,)), dma((n_dp,)),
            dma((PARTS, 2)), dma((PARTS, 2)), dma((2,)), dma((2,)),
            dma((PARTS, 2)), dma((PARTS, 2)), dma((2,)), dma((2,)),
        ],
        compiler_params=pltpu.CompilerParams(
            collective_id=0, has_side_effects=True, vmem_limit_bytes=50 * 1024 * 1024
        ),
        cost_estimate=pl.CostEstimate(
            flops=2 * width * slots * (rows + span * band),
            bytes_accessed=2 * width * (rows + cols * (band + 2 * REACH)),
            transcendentals=span * slots,
        ),
    )(embeddings, winners.reshape(1, rows))

    step = 8 if cols % 8 == 0 else cols
    return pl.pallas_call(
        finish_kernel,
        grid=(cols // step,),
        out_shape=(
            jax.ShapeDtypeStruct((cols, band, width), f32),
            jax.ShapeDtypeStruct((cols, band, width), bf16),
        ),
        in_specs=[
            pl.BlockSpec((step, band + 2 * REACH, width), lambda i: (i, 0, 0)),
            pl.BlockSpec((3, step, band), lambda i: (0, i, 0)),
            pl.BlockSpec((step, band, width), lambda i: (i, 0, 0)),
        ],
        out_specs=(
            pl.BlockSpec((step, band, width), lambda i: (i, 0, 0)),
            pl.BlockSpec((step, band, width), lambda i: (i, 0, 0)),
        ),
        compiler_params=pltpu.CompilerParams(vmem_limit_bytes=32 * 1024 * 1024),
    )(ext, den, codebook)


def solution(mesh):
    placed = (P("dp", None), P("dp"), P("dp", "map", None))
    return jax.shard_map(
        on_device,
        mesh=mesh,
        in_specs=placed,
        out_specs=(P("dp", "map", None), P("dp", "map", None)),
        check_vma=False,
    )
```

```python
import functools

import jax
import jax.numpy as jnp
from jax import lax
from jax.experimental import pallas as pl
from jax.experimental.pallas import tpu as pltpu
from jax.sharding import PartitionSpec as P

REACH = 16
SIGMA = float(REACH) / 2.0
HALVES = 2
MESH = pl.DeviceIdType.MESH
NT = (((1,), (1,)), ((), ()))


def iota(shape, dim):
    return lax.broadcasted_iota(jnp.int32, shape, dim)


def over(values, size):
    if size & (size - 1) == 0:
        return lax.shift_right_logical(values, jnp.int32(size.bit_length() - 1))
    return values // size


def weight(gap):
    apart = gap / SIGMA
    return jnp.where(jnp.abs(gap) <= REACH, jnp.exp(-0.5 * apart * apart) / SIGMA, 0.0)


def exchange_kernel(
    dims, emb_hbm, win_ref, ext_ref, den_ref,
    emb, rank, tags, x_out, x_in, k_out, k_in, cw, rm, mix, acc, h_out, h_in, d_out, d_in, d_own, y_out, t1, m_in,
    dm_in, e_sem, x_ss, x_rs, k_ss, k_rs, h_ss, h_rs, d_ss, d_rs, y_ss, y_rs, m_ss, m_rs, dm_ss, dm_rs,
):
    n_dp, n_map, cap, cols, band, rows, width = dims
    part = width // HALVES
    edge = REACH * band
    groups = cols // REACH
    pairs = n_dp // 2
    me = lax.axis_index("dp")
    mm = lax.axis_index("map")
    pair, mine = me // 2, me % 2
    mate = 2 * pair + 1 - mine
    left, right = lax.rem(me + n_dp - 2, n_dp), lax.rem(me + 2, n_dp)
    up, down = lax.rem(mm + n_map - 1, n_map), lax.rem(mm + 1, n_map)
    has_dp = (pair > 0, pair < pairs - 1)
    has_map = (mm > 0, mm < n_map - 1)

    fetch = pltpu.make_async_copy(emb_hbm, emb, e_sem)
    fetch.start()
    barrier = pltpu.get_barrier_semaphore()
    for k in range(1, n_dp):
        pl.semaphore_signal(
            barrier, inc=1, device_id=(lax.rem(me + k, n_dp), mm), device_id_type=MESH
        )
    for other in (up, down):
        pl.semaphore_signal(barrier, inc=1, device_id=(me, other), device_id_type=MESH)

    win = win_ref[...]
    column = over(win, band * n_map)
    row_of = win - column * (band * n_map) - mm * band
    target = over(column, cols)
    local = column - target * cols
    inside = (row_of >= 0) & (row_of < band)
    target = jnp.where(inside, target, -1)
    which = iota((16, rows), 0)
    tags[...] = jnp.where(
        which == 0,
        local.astype(jnp.float32),
        jnp.where(which == 1, row_of.astype(jnp.float32), jnp.where(which == 2, 1.0, 0.0)),
    ).astype(jnp.bfloat16)
    step = 256
    upper = jnp.where(iota((step, step), 0) <= iota((step, step), 1), 1.0, 0.0).astype(jnp.bfloat16)
    hits = jnp.where(target == iota((n_dp, rows), 0), 1.0, 0.0)
    carry = jnp.zeros((n_dp, 1), jnp.float32)
    for j in range(rows // step):
        hit = hits[:, j * step : (j + 1) * step]
        count = jnp.dot(hit.astype(jnp.bfloat16), upper, preferred_element_type=jnp.float32) + carry
        carry = count[:, step - 1 : step]
        rank[:, j * step : (j + 1) * step] = jnp.where(hit > 0.0, count - 1.0, -1.0).astype(jnp.int32)

    fetch.wait()
    pl.semaphore_wait(barrier, n_dp + 1)

    def plane(s):
        half = (s + 1) // 2
        return lax.rem(pair + pairs // 2 + half * (1 - 2 * (s % 2)), pairs)

    def place(s, sender):
        return pl.ds(pl.multiple_of((2 * s + sender) * cap, cap), cap)

    def x_copy(s, tile, to, sender):
        return pltpu.make_async_remote_copy(
            src_ref=x_out.at[s, to, tile],
            dst_ref=x_in.at[tile, place(s, sender), :],
            send_sem=x_ss.at[s, to, tile],
            recv_sem=x_rs.at[s, sender, tile],
            device_id=(2 * plane(s) + to, mm),
            device_id_type=MESH,
        )

    def k_copy(s, tile, to, sender):
        return pltpu.make_async_remote_copy(
            src_ref=k_out.at[s, tile],
            dst_ref=k_in.at[s, sender, tile],
            send_sem=k_ss.at[s, to, tile],
            recv_sem=k_rs.at[s, sender, tile],
            device_id=(2 * plane(s) + to, mm),
            device_id_type=MESH,
        )

    def pick(s, tile):
        to = 2 * plane(s) + tile
        chosen = jnp.where(rank[pl.ds(to, 1), :] == iota((cap, rows), 0), 1.0, 0.0).astype(jnp.bfloat16)
        packed = jnp.dot(chosen, emb[...], preferred_element_type=jnp.float32).astype(jnp.bfloat16)
        keys = lax.dot_general(tags[...], chosen, NT, preferred_element_type=jnp.float32)
        k_out[s, tile] = keys.astype(jnp.bfloat16)
        for h in range(HALVES):
            x_out[s, h, tile] = packed[:, h * part : (h + 1) * part]

    last = pairs - 1

    def send(i, none):
        s, tile = i // 2, i % 2
        pick(s, tile)

        @pl.when(s < last)
        def _():
            for to in range(2):
                k_copy(s, tile, to, mine).start()
                x_copy(s, tile, to, mine).start()

        @pl.when(s == last)
        def _():
            k_copy(s, tile, 1 - mine, mine).start()
            x_copy(s, tile, 1 - mine, mine).start()
            k_in[s, mine, tile] = k_out[s, tile]
            x_in[tile, place(s, mine), :] = x_out[s, mine, tile]

        return none

    lax.fori_loop(0, 2 * pairs, send, 0)
    acc[...] = jnp.zeros_like(acc)

    span = cols + 2 * REACH

    def take(s, senders):
        for sender in senders:
            for tile in range(2):
                k_copy(s, tile, 1 - mine, sender).wait_recv()
                x_copy(s, tile, 1 - mine, sender).wait_recv()
        for sender in range(2):
            for tile in range(2):
                key = k_in[s, sender, tile].astype(jnp.float32)
                gap = (iota((span, cap), 0) - REACH).astype(jnp.float32) - key[0:1, :]
                cw[tile, s, :, sender * cap : (sender + 1) * cap] = weight(gap) * key[2:3, :]
                rm[tile, s, :, sender * cap : (sender + 1) * cap] = jnp.where(
                    iota((band, cap), 0).astype(jnp.float32) == key[1:2, :], 1.0, 0.0
                ).astype(jnp.bfloat16)

    def contract(s, tile, g):
        lines = rm[tile, s]
        for i in range(REACH):
            line = jnp.broadcast_to(cw[tile, s, pl.ds(g * REACH + i, 1), :], (band, 2 * cap))
            mix[i * band : (i + 1) * band, :] = line.astype(jnp.bfloat16) * lines
        acc[tile * groups + g] += jnp.dot(
            mix[...],
            x_in[tile, pl.ds(pl.multiple_of(2 * s * cap, 2 * cap), 2 * cap), :],
            preferred_element_type=jnp.float32,
        )

    def add_step(s):
        def one(i, none):
            contract(s, i // (groups + 2), i % (groups + 2))
            return none

        lax.fori_loop(0, 2 * (groups + 2), one, 0)

    take(last, (1 - mine,))
    add_step(last)

    def middle_steps(s, none):
        take(s, (0, 1))
        add_step(s)
        return none

    lax.fori_loop(0, last - 1, middle_steps, 0)
    final = last - 1
    take(final, (0, 1))

    def h_copy(side):
        return pltpu.make_async_remote_copy(
            src_ref=h_out.at[side],
            dst_ref=h_in.at[1 - side],
            send_sem=h_ss.at[side],
            recv_sem=h_rs.at[1 - side],
            device_id=((left, right)[side], mm),
            device_id_type=MESH,
        )

    def d_copy(side):
        return pltpu.make_async_remote_copy(
            src_ref=d_out.at[side],
            dst_ref=d_in.at[1 - side],
            send_sem=d_ss.at[side],
            recv_sem=d_rs.at[1 - side],
            device_id=((left, right)[side], mm),
            device_id_type=MESH,
        )

    def y_copy(slot, cg):
        return pltpu.make_async_remote_copy(
            src_ref=y_out.at[slot],
            dst_ref=t1.at[cg, mine],
            send_sem=y_ss.at[slot],
            recv_sem=y_rs.at[slot],
            device_id=(mate, mm),
            device_id_type=MESH,
        )

    def m_copy(side, cg, h):
        start = 0 if side == 0 else band - REACH
        return pltpu.make_async_remote_copy(
            src_ref=t1.at[cg, h, :, pl.ds(start, REACH), :],
            dst_ref=m_in.at[1 - side, cg, h],
            send_sem=m_ss.at[side, cg, h],
            recv_sem=m_rs.at[1 - side, cg, h],
            device_id=(me, (up, down)[side]),
            device_id_type=MESH,
        )

    def m_start(cg, h):
        for side in range(2):
            @pl.when(has_map[side])
            def _(side=side):
                m_copy(side, cg, h).start()

    def dm_copy(side):
        return pltpu.make_async_remote_copy(
            src_ref=d_own,
            dst_ref=dm_in.at[1 - side],
            send_sem=dm_ss.at[side],
            recv_sem=dm_rs.at[1 - side],
            device_id=(me, (up, down)[side]),
            device_id_type=MESH,
        )

    for side in range(2):
        contract(final, side, 0 if side == 0 else groups + 1)
        h_out[side] = acc[0 if side == 0 else 2 * groups + 1].astype(jnp.bfloat16)

        @pl.when(has_dp[side])
        def _(side=side):
            h_copy(side).start()

    def inner(i, none):
        tile = i // groups
        contract(final, tile, i % groups + 2 * (1 - tile))
        return none

    lax.fori_loop(0, 2 * groups, inner, 0)
    block = (REACH, band, part)
    for m in range(groups - 1):
        y_out[m] = acc[2 + m + (1 - mine) * (groups - 1)].astype(jnp.bfloat16).reshape(block)
        y_copy(m, m + mine).start()
        t1[m + 1 - mine, mine] = acc[2 + m + mine * (groups - 1)].astype(jnp.bfloat16).reshape(block)
        m_start(m + 1 - mine, mine)
    contract(final, 0, 1)
    contract(final, 1, groups)

    totals = []
    for tile in range(2):
        total = jnp.zeros((span, band), jnp.float32)
        for s in range(pairs):
            total += lax.dot_general(
                cw[tile, s].astype(jnp.bfloat16), rm[tile, s], NT, preferred_element_type=jnp.float32
            )
        totals.append(total)
    d_out[0] = totals[0][:REACH]
    d_out[1] = totals[1][REACH + cols :]
    d_own[...] = jnp.where(
        mine == 0, totals[0][REACH : REACH + cols], totals[1][REACH : REACH + cols]
    )
    d_own[pl.ds(pl.multiple_of((1 - mine) * (cols - REACH), 8), REACH), :] += jnp.where(
        mine == 0, totals[1][:REACH], totals[0][REACH + cols :]
    )
    for side in range(2):
        @pl.when(has_dp[side])
        def _(side=side):
            d_copy(side).start()

    for side in range(2):
        @pl.when(has_dp[side])
        def _(side=side):
            h_copy(1 - side).wait_recv()
            acc[1 if side == 0 else 2 * groups] += h_in[side].astype(jnp.float32)

    tip = groups - 1
    y_out[tip] = acc[1 + (1 - mine) * (2 * groups - 1)].astype(jnp.bfloat16).reshape(block)
    y_copy(tip, (1 - mine) * (groups - 1)).start()
    own_tip = mine * (groups - 1)
    t1[own_tip, mine] = acc[1 + mine * (2 * groups - 1)].astype(jnp.bfloat16).reshape(block)
    m_start(own_tip, mine)

    for side in range(2):
        @pl.when(has_dp[side])
        def _(side=side):
            d_copy(1 - side).wait_recv()

        @pl.when(has_dp[side] & (mine == side))
        def _(side=side):
            base = 0 if side == 0 else cols - REACH
            d_own[pl.ds(base, REACH), :] += d_in[side]

    for side in range(2):
        @pl.when(has_map[side])
        def _(side=side):
            dm_copy(side).start()

    for m in range(groups - 1):
        y_copy(m, m + mine).wait_recv()
        m_start(m + 1 - mine, 1 - mine)
    y_copy(tip, own_tip).wait_recv()
    m_start(own_tip, 1 - mine)

    for cg in range(groups):
        for h in range(HALVES):
            ext_ref[cg * REACH : (cg + 1) * REACH, REACH : REACH + band, h * part : (h + 1) * part] = t1[cg, h]
    den_ref[1] = d_own[...]

    for side in range(2):
        base = 0 if side == 0 else REACH + band

        @pl.when(has_map[side])
        def _(side=side, base=base):
            dm_copy(1 - side).wait_recv()
            den_ref[2 * side] = dm_in[side]
            for cg in range(groups):
                for h in range(HALVES):
                    m_copy(1 - side, cg, h).wait_recv()
                    ext_ref[
                        cg * REACH : (cg + 1) * REACH, base : base + REACH, h * part : (h + 1) * part
                    ] = m_in[side, cg, h]

        @pl.when(jnp.logical_not(has_map[side]))
        def _(side=side, base=base):
            den_ref[2 * side] = jnp.zeros((cols, band), jnp.float32)
            ext_ref[:, base : base + REACH, :] = jnp.zeros((cols, REACH, width), jnp.bfloat16)

    def sent(i, none):
        s, tile = i // 2, i % 2
        for to in range(2):
            @pl.when((s < last) | (mine != to))
            def _(to=to):
                k_copy(s, tile, to, mine).wait_send()
                x_copy(s, tile, to, mine).wait_send()

        return none

    lax.fori_loop(0, 2 * pairs, sent, 0)
    for cg in range(groups):
        y_copy(cg, 0).wait_send()
    for side in range(2):
        @pl.when(has_dp[side])
        def _(side=side):
            d_copy(side).wait_send()
            h_copy(side).wait_send()

        @pl.when(has_map[side])
        def _(side=side):
            dm_copy(side).wait_send()
            for cg in range(groups):
                for h in range(HALVES):
                    m_copy(side, cg, h).wait_send()


def finish_kernel(ext_ref, den_ref, book_ref, new_ref, copy_ref):
    count, band, width = book_ref.shape
    reach_band = ext_ref.shape[1]
    gap = iota((band, reach_band), 0) + REACH - iota((band, reach_band), 1)
    smooth = weight(gap.astype(jnp.float32)).astype(jnp.bfloat16)
    den = jnp.zeros((band, count), jnp.float32)
    apart = (iota((band, band), 0) - iota((band, band), 1)).astype(jnp.float32)
    for p in range(3):
        taps = weight(apart + float((1 - p) * band)).astype(jnp.bfloat16).astype(jnp.float32)
        den += lax.dot_general(
            taps, den_ref[p], NT, precision=lax.Precision.HIGHEST, preferred_element_type=jnp.float32
        )
    scale = 0.9 / (den + 1.0)
    for i in range(count):
        num = jnp.dot(smooth, ext_ref[i], preferred_element_type=jnp.float32)
        book = book_ref[i]
        new = 0.1 * book + (num + book) * scale[:, i : i + 1]
        new_ref[i] = new
        copy_ref[i] = new.astype(jnp.bfloat16)


def on_device(embeddings, winners, codebook):
    cols, band, width = codebook.shape
    n_dp = lax.axis_size("dp")
    n_map = lax.axis_size("map")
    rows = embeddings.shape[0]
    cap = max(2, 2 * rows // (n_dp * n_map))
    slots = n_dp * cap
    part = width // HALVES
    pairs = n_dp // 2
    groups = cols // REACH
    span = cols + 2 * REACH
    edge = REACH * band
    bf16, f32 = jnp.bfloat16, jnp.float32
    vmem = pl.BlockSpec(memory_space=pltpu.VMEM)
    dma = pltpu.SemaphoreType.DMA
    ext, den = pl.pallas_call(
        functools.partial(exchange_kernel, (n_dp, n_map, cap, cols, band, rows, width)),
        out_shape=(
            jax.ShapeDtypeStruct((cols, band + 2 * REACH, width), bf16),
            jax.ShapeDtypeStruct((3, cols, band), f32),
        ),
        in_specs=[pl.BlockSpec(memory_space=pl.ANY), vmem],
        out_specs=(vmem, vmem),
        scratch_shapes=[
            pltpu.VMEM((rows, width), bf16),
            pltpu.VMEM((n_dp, rows), jnp.int32),
            pltpu.VMEM((16, rows), bf16),
            pltpu.VMEM((pairs, HALVES, 2, cap, part), bf16),
            pltpu.VMEM((2, slots, part), bf16),
            pltpu.VMEM((pairs, 2, 16, cap), bf16),
            pltpu.VMEM((pairs, 2, 2, 16, cap), bf16),
            pltpu.VMEM((2, pairs, span, 2 * cap), f32),
            pltpu.VMEM((2, pairs, band, 2 * cap), bf16),
            pltpu.VMEM((edge, 2 * cap), bf16),
            pltpu.VMEM((2 * groups + 2, edge, part), f32),
            pltpu.VMEM((2, edge, part), bf16),
            pltpu.VMEM((2, edge, part), bf16),
            pltpu.VMEM((2, REACH, band), f32),
            pltpu.VMEM((2, REACH, band), f32),
            pltpu.VMEM((cols, band), f32),
            pltpu.VMEM((groups, REACH, band, part), bf16),
            pltpu.VMEM((groups, HALVES, REACH, band, part), bf16),
            pltpu.VMEM((2, groups, HALVES, REACH, REACH, part), bf16),
            pltpu.VMEM((2, cols, band), f32),
            dma,
            dma((pairs, 2, 2)), dma((pairs, 2, 2)), dma((pairs, 2, 2)), dma((pairs, 2, 2)),
            dma((2,)), dma((2,)), dma((2,)), dma((2,)), dma((groups,)), dma((groups,)),
            dma((2, groups, HALVES)), dma((2, groups, HALVES)), dma((2,)), dma((2,)),
        ],
        compiler_params=pltpu.CompilerParams(
            collective_id=0, has_side_effects=True, vmem_limit_bytes=50 * 1024 * 1024
        ),
        cost_estimate=pl.CostEstimate(
            flops=2 * width * slots * (rows + span * band),
            bytes_accessed=2 * width * (rows + cols * (band + 2 * REACH)),
            transcendentals=span * slots,
        ),
    )(embeddings, winners.reshape(1, rows))

    step = 8 if cols % 8 == 0 else cols
    return pl.pallas_call(
        finish_kernel,
        grid=(cols // step,),
        out_shape=(
            jax.ShapeDtypeStruct((cols, band, width), f32),
            jax.ShapeDtypeStruct((cols, band, width), bf16),
        ),
        in_specs=[
            pl.BlockSpec((step, band + 2 * REACH, width), lambda i: (i, 0, 0)),
            pl.BlockSpec((3, step, band), lambda i: (0, i, 0)),
            pl.BlockSpec((step, band, width), lambda i: (i, 0, 0)),
        ],
        out_specs=(
            pl.BlockSpec((step, band, width), lambda i: (i, 0, 0)),
            pl.BlockSpec((step, band, width), lambda i: (i, 0, 0)),
        ),
        compiler_params=pltpu.CompilerParams(vmem_limit_bytes=32 * 1024 * 1024),
    )(ext, den, codebook)


def solution(mesh):
    placed = (P("dp", None), P("dp"), P("dp", "map", None))
    return jax.shard_map(
        on_device,
        mesh=mesh,
        in_specs=placed,
        out_specs=(P("dp", "map", None), P("dp", "map", None)),
        check_vma=False,
    )
```

```python
import functools

import jax
import jax.numpy as jnp
from jax import lax
from jax.experimental import pallas as pl
from jax.experimental.pallas import tpu as pltpu
from jax.sharding import PartitionSpec as P

REACH = 16
SIGMA = float(REACH) / 2.0
HALVES = 2
MESH = pl.DeviceIdType.MESH
NT = (((1,), (1,)), ((), ()))


def iota(shape, dim):
    return lax.broadcasted_iota(jnp.int32, shape, dim)


def over(values, size):
    if size & (size - 1) == 0:
        return lax.shift_right_logical(values, jnp.int32(size.bit_length() - 1))
    return values // size


def weight(gap):
    apart = gap / SIGMA
    return jnp.where(jnp.abs(gap) <= REACH, jnp.exp(-0.5 * apart * apart) / SIGMA, 0.0)


def exchange_kernel(
    dims, emb_hbm, win_ref, ext_ref, den_ref,
    emb, rank, tags, x_out, x_in, k_out, k_in, oc, rm, mix, acc, raw, h_in, mid, tips, d_ext, d_own, y_out, t1, m_in,
    dm_in, e_sem, x_ss, x_rs, k_ss, k_rs, h_ss, h_rs, d_ss, d_rs, y_ss, y_rs, m_ss, m_rs, dm_ss, dm_rs,
):
    n_dp, n_map, cap, cols, band, rows, width = dims
    part = width // HALVES
    groups = cols // REACH
    pairs = n_dp // 2
    me = lax.axis_index("dp")
    mm = lax.axis_index("map")
    pair, mine = me // 2, me % 2
    mate = 2 * pair + 1 - mine
    left, right = lax.rem(me + n_dp - 2, n_dp), lax.rem(me + 2, n_dp)
    up, down = lax.rem(mm + n_map - 1, n_map), lax.rem(mm + 1, n_map)
    has_dp = (pair > 0, pair < pairs - 1)
    has_map = (mm > 0, mm < n_map - 1)

    fetch = pltpu.make_async_copy(emb_hbm, emb, e_sem)
    fetch.start()
    barrier = pltpu.get_barrier_semaphore()
    for k in range(1, n_dp):
        pl.semaphore_signal(
            barrier, inc=1, device_id=(lax.rem(me + k, n_dp), mm), device_id_type=MESH
        )
    for other in (up, down):
        pl.semaphore_signal(barrier, inc=1, device_id=(me, other), device_id_type=MESH)

    win = win_ref[...]
    column = over(win, band * n_map)
    row_of = win - column * (band * n_map) - mm * band
    target = over(column, cols)
    local = column - target * cols
    inside = (row_of >= 0) & (row_of < band)
    target = jnp.where(inside, target, -1)
    tags[...] = (local * band + row_of + 1).astype(jnp.float32)
    step = 256
    upper = jnp.where(iota((step, step), 0) <= iota((step, step), 1), 1.0, 0.0).astype(jnp.bfloat16)
    hits = jnp.where(target == iota((n_dp, rows), 0), 1.0, 0.0)
    carry = jnp.zeros((n_dp, 1), jnp.float32)
    for j in range(rows // step):
        hit = hits[:, j * step : (j + 1) * step]
        count = jnp.dot(hit.astype(jnp.bfloat16), upper, preferred_element_type=jnp.float32) + carry
        carry = count[:, step - 1 : step]
        rank[:, j * step : (j + 1) * step] = jnp.where(hit > 0.0, count - 1.0, -1.0).astype(jnp.int32)

    fetch.wait()
    pl.semaphore_wait(barrier, n_dp + 1)

    def plane(s):
        half = (s + 1) // 2
        return lax.rem(pair + pairs // 2 + half * (1 - 2 * (s % 2)), pairs)

    def place(s, sender):
        return pl.ds(pl.multiple_of((2 * s + sender) * cap, cap), cap)

    def x_copy(s, tile, to, sender):
        return pltpu.make_async_remote_copy(
            src_ref=x_out.at[s, to, tile],
            dst_ref=x_in.at[tile, place(s, sender), :],
            send_sem=x_ss.at[s, to, tile],
            recv_sem=x_rs.at[s, sender, tile],
            device_id=(2 * plane(s) + to, mm),
            device_id_type=MESH,
        )

    def k_copy(s, tile, to, sender):
        return pltpu.make_async_remote_copy(
            src_ref=k_out.at[s, tile],
            dst_ref=k_in.at[s, sender, tile],
            send_sem=k_ss.at[s, to, tile],
            recv_sem=k_rs.at[s, sender, tile],
            device_id=(2 * plane(s) + to, mm),
            device_id_type=MESH,
        )

    def pick(s, tile):
        to = 2 * plane(s) + tile
        match = rank[pl.ds(to, 1), :] == iota((cap, rows), 0)
        chosen = jnp.where(match, 1.0, 0.0).astype(jnp.bfloat16)
        packed = jnp.dot(chosen, emb[...], preferred_element_type=jnp.float32).astype(jnp.bfloat16)
        key = jnp.sum(jnp.where(match, tags[...], 0.0), axis=1, keepdims=True)
        turned = jnp.where(iota((cap, cap), 0) == iota((cap, cap), 1), key, 0.0)
        k_out[s, tile] = jnp.broadcast_to(jnp.sum(turned, axis=0, keepdims=True), (8, cap))
        for h in range(HALVES):
            x_out[s, h, tile] = packed[:, h * part : (h + 1) * part]

    last = pairs - 1

    def send(i, none):
        s, tile = i // 2, i % 2
        pick(s, tile)

        @pl.when(s < last)
        def _():
            for to in range(2):
                k_copy(s, tile, to, mine).start()
                x_copy(s, tile, to, mine).start()

        @pl.when(s == last)
        def _():
            k_copy(s, tile, 1 - mine, mine).start()
            x_copy(s, tile, 1 - mine, mine).start()
            k_in[s, mine, tile] = k_out[s, tile]
            x_in[tile, place(s, mine), :] = x_out[s, mine, tile]

        return none

    lax.fori_loop(0, 2 * pairs, send, 0)
    acc[...] = jnp.zeros_like(acc)

    lot = min(band, 1024 // cols)
    lots = band // lot

    def take(s, senders):
        for sender in senders:
            for tile in range(2):
                k_copy(s, tile, 1 - mine, sender).wait_recv()
                x_copy(s, tile, 1 - mine, sender).wait_recv()
        for sender in range(2):
            for tile in range(2):
                key = k_in[s, sender, tile][0:1, :].astype(jnp.int32) - 1
                at = over(key, band)
                lanes = slice(sender * cap, (sender + 1) * cap)
                oc[tile, s, :, lanes] = jnp.where(iota((cols, cap), 0) == at, 1.0, 0.0).astype(jnp.bfloat16)
                rm[tile, s, :, lanes] = jnp.where(iota((band, cap), 0) == key - at * band, 1.0, 0.0)

    def contract(s, tile, j):
        lines = oc[tile, s]
        for i in range(lot):
            line = jnp.broadcast_to(rm[tile, s, pl.ds(j * lot + i, 1), :], (cols, 2 * cap))
            mix[i * cols : (i + 1) * cols, :] = line.astype(jnp.bfloat16) * lines
        acc[tile, pl.ds(pl.multiple_of(j * lot * cols, lot * cols), lot * cols), :] += jnp.dot(
            mix[...],
            x_in[tile, pl.ds(pl.multiple_of(2 * s * cap, 2 * cap), 2 * cap), :],
            preferred_element_type=jnp.float32,
        )

    def add_step(s):
        def one(i, none):
            contract(s, i // lots, i % lots)
            return none

        lax.fori_loop(0, 2 * lots, one, 0)

    take(last, (1 - mine,))
    add_step(last)

    def middle_steps(s, none):
        take(s, (0, 1))
        add_step(s)
        return none

    lax.fori_loop(0, last, middle_steps, 0)

    def h_copy(side):
        return pltpu.make_async_remote_copy(
            src_ref=raw.at[side, :, pl.ds(0 if side == 0 else cols - REACH, REACH), :],
            dst_ref=h_in.at[1 - side],
            send_sem=h_ss.at[side],
            recv_sem=h_rs.at[1 - side],
            device_id=((left, right)[side], mm),
            device_id_type=MESH,
        )

    def d_copy(side):
        return pltpu.make_async_remote_copy(
            src_ref=d_ext.at[pl.ds(REACH if side == 0 else 2 * cols, REACH), :],
            dst_ref=d_ext.at[pl.ds(REACH + 2 * cols if side == 0 else 0, REACH), :],
            send_sem=d_ss.at[side],
            recv_sem=d_rs.at[1 - side],
            device_id=((left, right)[side], mm),
            device_id_type=MESH,
        )

    def y_copy(slot, cg):
        return pltpu.make_async_remote_copy(
            src_ref=y_out.at[slot],
            dst_ref=t1.at[cg, mine],
            send_sem=y_ss.at[slot],
            recv_sem=y_rs.at[slot],
            device_id=(mate, mm),
            device_id_type=MESH,
        )

    def m_copy(side, cg, h):
        start = 0 if side == 0 else band - REACH
        return pltpu.make_async_remote_copy(
            src_ref=t1.at[cg, h, :, pl.ds(start, REACH), :],
            dst_ref=m_in.at[1 - side, cg, h],
            send_sem=m_ss.at[side, cg, h],
            recv_sem=m_rs.at[1 - side, cg, h],
            device_id=(me, (up, down)[side]),
            device_id_type=MESH,
        )

    def m_start(cg, h):
        for side in range(2):
            @pl.when(has_map[side])
            def _(side=side):
                m_copy(side, cg, h).start()

    def dm_copy(side):
        return pltpu.make_async_remote_copy(
            src_ref=d_own,
            dst_ref=dm_in.at[1 - side],
            send_sem=dm_ss.at[side],
            recv_sem=dm_rs.at[1 - side],
            device_id=(me, (up, down)[side]),
            device_id_type=MESH,
        )

    for side in range(2):
        raw[side] = acc[side].astype(jnp.bfloat16).reshape(band, cols, part)

        @pl.when(has_dp[side])
        def _(side=side):
            h_copy(side).start()

        @pl.when(jnp.logical_not(has_dp[side]))
        def _(side=side):
            h_in[side] = jnp.zeros((band, REACH, part), jnp.bfloat16)
            d_ext[pl.ds(0 if side == 0 else REACH + 2 * cols, REACH), :] = jnp.zeros((REACH, band), jnp.float32)

    for tile in range(2):
        total = jnp.zeros((cols, band), jnp.float32)
        for s in range(pairs):
            total += lax.dot_general(
                oc[tile, s], rm[tile, s].astype(jnp.bfloat16), NT, preferred_element_type=jnp.float32
            )
        d_ext[REACH + tile * cols : REACH + (tile + 1) * cols, :] = total
    for side in range(2):
        @pl.when(has_dp[side])
        def _(side=side):
            d_copy(side).start()

    def smooth(taps, parts_of, out):
        size = taps.shape[0]

        def rows_at(i, none):
            ext = jnp.concatenate(
                [jnp.concatenate(parts_of(4 * i + j), axis=0) for j in range(4)], axis=1
            )
            got = jnp.dot(taps, ext, preferred_element_type=jnp.float32)
            for j in range(4):
                out[pl.ds(pl.multiple_of((4 * i + j) * size, size), size), :] = got[
                    :, j * part : (j + 1) * part
                ]
            return none

        lax.fori_loop(0, band // 4, rows_at, 0)

    def share(low, high):
        first = mine == 0
        return (
            jnp.where(first, low, high).astype(jnp.bfloat16),
            jnp.where(first, high, low).astype(jnp.bfloat16),
        )

    inner = groups - 1
    if inner:
        size = 2 * inner * REACH
        gap = iota((size, 2 * cols), 0) + REACH - iota((size, 2 * cols), 1)
        taps = weight(gap.astype(jnp.float32)).astype(jnp.bfloat16)
        smooth(taps, lambda r: [raw[0, r], raw[1, r]], mid)
        for m in range(inner):
            for i in range(REACH):
                kept, given = share(
                    mid[pl.ds(m * REACH + i, band, stride=size), :],
                    mid[pl.ds((m + inner) * REACH + i, band, stride=size), :],
                )
                t1[m + 1 - mine, mine, i] = kept
                y_out[m, i] = given
            y_copy(m, m + mine).start()
            m_start(m + 1 - mine, mine)

    size = 2 * REACH
    reached = 2 * cols + 2 * REACH
    place_of = iota((size, reached), 0)
    place_of = jnp.where(place_of < REACH, place_of, place_of + 2 * cols - 2 * REACH)
    taps = weight((place_of + REACH - iota((size, reached), 1)).astype(jnp.float32)).astype(jnp.bfloat16)
    for side in range(2):
        @pl.when(has_dp[side])
        def _(side=side):
            h_copy(1 - side).wait_recv()

    smooth(taps, lambda r: [h_in[0, r], raw[0, r], raw[1, r], h_in[1, r]], tips)
    tip = groups - 1
    own_tip = mine * (groups - 1)
    for i in range(REACH):
        kept, given = share(
            tips[pl.ds(i, band, stride=size), :], tips[pl.ds(REACH + i, band, stride=size), :]
        )
        t1[own_tip, mine, i] = kept
        y_out[tip, i] = given
    y_copy(tip, (1 - mine) * (groups - 1)).start()
    m_start(own_tip, mine)

    for side in range(2):
        @pl.when(has_dp[side])
        def _(side=side):
            d_copy(1 - side).wait_recv()

    gap = iota((cols, reached), 0) + mine * cols + REACH - iota((cols, reached), 1)
    d_own[...] = jnp.dot(
        weight(gap.astype(jnp.float32)).astype(jnp.bfloat16).astype(jnp.float32),
        d_ext[...],
        precision=lax.Precision.HIGHEST,
        preferred_element_type=jnp.float32,
    )
    for side in range(2):
        @pl.when(has_map[side])
        def _(side=side):
            dm_copy(side).start()

    for m in range(groups - 1):
        y_copy(m, m + mine).wait_recv()
        m_start(m + 1 - mine, 1 - mine)
    y_copy(tip, own_tip).wait_recv()
    m_start(own_tip, 1 - mine)

    for cg in range(groups):
        for h in range(HALVES):
            ext_ref[cg * REACH : (cg + 1) * REACH, REACH : REACH + band, h * part : (h + 1) * part] = t1[cg, h]
    den_ref[1] = d_own[...]

    for side in range(2):
        base = 0 if side == 0 else REACH + band

        @pl.when(has_map[side])
        def _(side=side, base=base):
            dm_copy(1 - side).wait_recv()
            den_ref[2 * side] = dm_in[side]
            for cg in range(groups):
                for h in range(HALVES):
                    m_copy(1 - side, cg, h).wait_recv()
                    ext_ref[
                        cg * REACH : (cg + 1) * REACH, base : base + REACH, h * part : (h + 1) * part
                    ] = m_in[side, cg, h]

        @pl.when(jnp.logical_not(has_map[side]))
        def _(side=side, base=base):
            den_ref[2 * side] = jnp.zeros((cols, band), jnp.float32)
            ext_ref[:, base : base + REACH, :] = jnp.zeros((cols, REACH, width), jnp.bfloat16)

    def sent(i, none):
        s, tile = i // 2, i % 2
        for to in range(2):
            @pl.when((s < last) | (mine != to))
            def _(to=to):
                k_copy(s, tile, to, mine).wait_send()
                x_copy(s, tile, to, mine).wait_send()

        return none

    lax.fori_loop(0, 2 * pairs, sent, 0)
    for cg in range(groups):
        y_copy(cg, 0).wait_send()
    for side in range(2):
        @pl.when(has_dp[side])
        def _(side=side):
            d_copy(side).wait_send()
            h_copy(side).wait_send()

        @pl.when(has_map[side])
        def _(side=side):
            dm_copy(side).wait_send()
            for cg in range(groups):
                for h in range(HALVES):
                    m_copy(side, cg, h).wait_send()


def finish_kernel(ext_ref, den_ref, book_ref, new_ref, copy_ref):
    count, band, width = book_ref.shape
    reach_band = ext_ref.shape[1]
    gap = iota((band, reach_band), 0) + REACH - iota((band, reach_band), 1)
    smooth = weight(gap.astype(jnp.float32)).astype(jnp.bfloat16)
    den = jnp.zeros((band, count), jnp.float32)
    apart = (iota((band, band), 0) - iota((band, band), 1)).astype(jnp.float32)
    for p in range(3):
        taps = weight(apart + float((1 - p) * band)).astype(jnp.bfloat16).astype(jnp.float32)
        den += lax.dot_general(
            taps, den_ref[p], NT, precision=lax.Precision.HIGHEST, preferred_element_type=jnp.float32
        )
    scale = 0.9 / (den + 1.0)
    for i in range(count):
        num = jnp.dot(smooth, ext_ref[i], preferred_element_type=jnp.float32)
        book = book_ref[i]
        new = 0.1 * book + (num + book) * scale[:, i : i + 1]
        new_ref[i] = new
        copy_ref[i] = new.astype(jnp.bfloat16)


def on_device(embeddings, winners, codebook):
    cols, band, width = codebook.shape
    n_dp = lax.axis_size("dp")
    n_map = lax.axis_size("map")
    rows = embeddings.shape[0]
    cap = max(2, 2 * rows // (n_dp * n_map))
    slots = n_dp * cap
    part = width // HALVES
    pairs = n_dp // 2
    groups = cols // REACH
    bf16, f32 = jnp.bfloat16, jnp.float32
    vmem = pl.BlockSpec(memory_space=pltpu.VMEM)
    dma = pltpu.SemaphoreType.DMA
    ext, den = pl.pallas_call(
        functools.partial(exchange_kernel, (n_dp, n_map, cap, cols, band, rows, width)),
        out_shape=(
            jax.ShapeDtypeStruct((cols, band + 2 * REACH, width), bf16),
            jax.ShapeDtypeStruct((3, cols, band), f32),
        ),
        in_specs=[pl.BlockSpec(memory_space=pl.ANY), vmem],
        out_specs=(vmem, vmem),
        scratch_shapes=[
            pltpu.VMEM((rows, width), bf16),
            pltpu.VMEM((n_dp, rows), jnp.int32),
            pltpu.VMEM((1, rows), f32),
            pltpu.VMEM((pairs, HALVES, 2, cap, part), bf16),
            pltpu.VMEM((2, slots, part), bf16),
            pltpu.VMEM((pairs, 2, 8, cap), f32),
            pltpu.VMEM((pairs, 2, 2, 8, cap), f32),
            pltpu.VMEM((2, pairs, cols, 2 * cap), bf16),
            pltpu.VMEM((2, pairs, band, 2 * cap), f32),
            pltpu.VMEM((min(band, 1024 // cols) * cols, 2 * cap), bf16),
            pltpu.VMEM((2, band * cols, part), f32),
            pltpu.VMEM((2, band, cols, part), bf16),
            pltpu.VMEM((2, band, REACH, part), bf16),
            pltpu.VMEM((band * max(1, 2 * (groups - 1)) * REACH, part), f32),
            pltpu.VMEM((band * 2 * REACH, part), f32),
            pltpu.VMEM((2 * cols + 2 * REACH, band), f32),
            pltpu.VMEM((cols, band), f32),
            pltpu.VMEM((groups, REACH, band, part), bf16),
            pltpu.VMEM((groups, HALVES, REACH, band, part), bf16),
            pltpu.VMEM((2, groups, HALVES, REACH, REACH, part), bf16),
            pltpu.VMEM((2, cols, band), f32),
            dma,
            dma((pairs, 2, 2)), dma((pairs, 2, 2)), dma((pairs, 2, 2)), dma((pairs, 2, 2)),
            dma((2,)), dma((2,)), dma((2,)), dma((2,)), dma((groups,)), dma((groups,)),
            dma((2, groups, HALVES)), dma((2, groups, HALVES)), dma((2,)), dma((2,)),
        ],
        compiler_params=pltpu.CompilerParams(
            collective_id=0, has_side_effects=True, vmem_limit_bytes=60 * 1024 * 1024
        ),
        cost_estimate=pl.CostEstimate(
            flops=2 * width * slots * (rows + cols * band),
            bytes_accessed=2 * width * (rows + cols * (band + 2 * REACH)),
            transcendentals=0,
        ),
    )(embeddings, winners.reshape(1, rows))

    step = 8 if cols % 8 == 0 else cols
    return pl.pallas_call(
        finish_kernel,
        grid=(cols // step,),
        out_shape=(
            jax.ShapeDtypeStruct((cols, band, width), f32),
            jax.ShapeDtypeStruct((cols, band, width), bf16),
        ),
        in_specs=[
            pl.BlockSpec((step, band + 2 * REACH, width), lambda i: (i, 0, 0)),
            pl.BlockSpec((3, step, band), lambda i: (0, i, 0)),
            pl.BlockSpec((step, band, width), lambda i: (i, 0, 0)),
        ],
        out_specs=(
            pl.BlockSpec((step, band, width), lambda i: (i, 0, 0)),
            pl.BlockSpec((step, band, width), lambda i: (i, 0, 0)),
        ),
        compiler_params=pltpu.CompilerParams(vmem_limit_bytes=60 * 1024 * 1024),
    )(ext, den, codebook)


def solution(mesh):
    placed = (P("dp", None), P("dp"), P("dp", "map", None))
    return jax.shard_map(
        on_device,
        mesh=mesh,
        in_specs=placed,
        out_specs=(P("dp", "map", None), P("dp", "map", None)),
        check_vma=False,
    )
```

```python
import functools

import jax
import jax.numpy as jnp
from jax import lax
from jax.experimental import pallas as pl
from jax.experimental.pallas import tpu as pltpu
from jax.sharding import PartitionSpec as P

REACH = 16
SIGMA = float(REACH) / 2.0
HALVES = 2
UNIT = REACH // 2
MESH = pl.DeviceIdType.MESH
NT = (((1,), (1,)), ((), ()))


def iota(shape, dim):
    return lax.broadcasted_iota(jnp.int32, shape, dim)


def over(values, size):
    if size & (size - 1) == 0:
        return lax.shift_right_logical(values, jnp.int32(size.bit_length() - 1))
    return values // size


def weight(gap):
    apart = gap / SIGMA
    return jnp.where(jnp.abs(gap) <= REACH, jnp.exp(-0.5 * apart * apart) / SIGMA, 0.0)


def exchange_kernel(
    dims, emb_hbm, win_ref, num_ref, scale_ref,
    emb, rank, tags, x_out, x_in, k_out, k_in, cw, rm, mix, acc, h_out, h_in, d_out, d_in, d_own, y_out, t1, m_in,
    dm_in, e_sem, x_ss, x_rs, k_ss, k_rs, h_ss, h_rs, d_ss, d_rs, y_ss, y_rs, m_ss, m_rs, dm_ss, dm_rs,
):
    n_dp, n_map, cap, cols, band, rows, width = dims
    part = width // HALVES
    unit = UNIT * band
    over_units = REACH // UNIT
    col_units = cols // UNIT
    spare = col_units - over_units
    span_units = col_units + 2 * over_units
    pairs = n_dp // 2
    me = lax.axis_index("dp")
    mm = lax.axis_index("map")
    pair, mine = me // 2, me % 2
    mate = 2 * pair + 1 - mine
    left, right = lax.rem(me + n_dp - 2, n_dp), lax.rem(me + 2, n_dp)
    up, down = lax.rem(mm + n_map - 1, n_map), lax.rem(mm + 1, n_map)
    has_dp = (pair > 0, pair < pairs - 1)
    has_map = (mm > 0, mm < n_map - 1)

    fetch = pltpu.make_async_copy(emb_hbm, emb, e_sem)
    fetch.start()
    barrier = pltpu.get_barrier_semaphore()
    for k in range(1, n_dp):
        pl.semaphore_signal(
            barrier, inc=1, device_id=(lax.rem(me + k, n_dp), mm), device_id_type=MESH
        )
    for other in (up, down):
        pl.semaphore_signal(barrier, inc=1, device_id=(me, other), device_id_type=MESH)

    win = win_ref[...]
    column = over(win, band * n_map)
    row_of = win - column * (band * n_map) - mm * band
    target = over(column, cols)
    local = column - target * cols
    inside = (row_of >= 0) & (row_of < band)
    target = jnp.where(inside, target, -1)
    tags[...] = (local * band + row_of + 1).astype(jnp.float32)
    step = 256
    upper = jnp.where(iota((step, step), 0) <= iota((step, step), 1), 1.0, 0.0).astype(jnp.bfloat16)
    hits = jnp.where(target == iota((n_dp, rows), 0), 1.0, 0.0)
    carry = jnp.zeros((n_dp, 1), jnp.float32)
    for j in range(rows // step):
        hit = hits[:, j * step : (j + 1) * step]
        count = jnp.dot(hit.astype(jnp.bfloat16), upper, preferred_element_type=jnp.float32) + carry
        carry = count[:, step - 1 : step]
        rank[:, j * step : (j + 1) * step] = jnp.where(hit > 0.0, count - 1.0, -1.0).astype(jnp.int32)

    fetch.wait()
    pl.semaphore_wait(barrier, n_dp + 1)

    def plane(s):
        half = (s + 1) // 2
        return lax.rem(pair + pairs // 2 + half * (1 - 2 * (s % 2)), pairs)

    def place(s, sender):
        return pl.ds(pl.multiple_of((2 * s + sender) * cap, cap), cap)

    def x_copy(s, tile, to, sender):
        return pltpu.make_async_remote_copy(
            src_ref=x_out.at[s, to, tile],
            dst_ref=x_in.at[tile, place(s, sender), :],
            send_sem=x_ss.at[s, to, tile],
            recv_sem=x_rs.at[s, sender, tile],
            device_id=(2 * plane(s) + to, mm),
            device_id_type=MESH,
        )

    def k_copy(s, tile, to, sender):
        return pltpu.make_async_remote_copy(
            src_ref=k_out.at[s, tile],
            dst_ref=k_in.at[s, sender, tile],
            send_sem=k_ss.at[s, to, tile],
            recv_sem=k_rs.at[s, sender, tile],
            device_id=(2 * plane(s) + to, mm),
            device_id_type=MESH,
        )

    def pick(s, tile):
        to = 2 * plane(s) + tile
        match = rank[pl.ds(to, 1), :] == iota((cap, rows), 0)
        chosen = jnp.where(match, 1.0, 0.0).astype(jnp.bfloat16)
        packed = jnp.dot(chosen, emb[...], preferred_element_type=jnp.float32).astype(jnp.bfloat16)
        key = jnp.sum(jnp.where(match, tags[...], 0.0), axis=1, keepdims=True)
        turned = jnp.where(iota((cap, cap), 0) == iota((cap, cap), 1), key, 0.0)
        k_out[s, tile] = jnp.broadcast_to(jnp.sum(turned, axis=0, keepdims=True), (8, cap))
        for h in range(HALVES):
            x_out[s, h, tile] = packed[:, h * part : (h + 1) * part]

    last = pairs - 1

    def send(i, none):
        s, tile = i // 2, i % 2
        pick(s, tile)

        @pl.when(s < last)
        def _():
            for to in range(2):
                k_copy(s, tile, to, mine).start()
                x_copy(s, tile, to, mine).start()

        @pl.when(s == last)
        def _():
            k_copy(s, tile, 1 - mine, mine).start()
            x_copy(s, tile, 1 - mine, mine).start()
            k_in[s, mine, tile] = k_out[s, tile]
            x_in[tile, place(s, mine), :] = x_out[s, mine, tile]

        return none

    lax.fori_loop(0, 2 * pairs, send, 0)
    acc[...] = jnp.zeros_like(acc)

    span = cols + 2 * REACH

    def take(s, senders):
        for sender in senders:
            for tile in range(2):
                k_copy(s, tile, 1 - mine, sender).wait_recv()
                x_copy(s, tile, 1 - mine, sender).wait_recv()
        for sender in range(2):
            for tile in range(2):
                key = k_in[s, sender, tile][0:1, :].astype(jnp.int32) - 1
                at = over(key, band)
                gap = (iota((span, cap), 0) - REACH - at).astype(jnp.float32)
                lanes = slice(sender * cap, (sender + 1) * cap)
                cw[tile, s, :, lanes] = weight(gap)
                rm[tile, s, :, lanes] = jnp.where(
                    iota((band, cap), 0) == key - at * band, 1.0, 0.0
                ).astype(jnp.bfloat16)

    def contract(s, tile, g, count):
        lines = rm[tile, s]
        for i in range(UNIT * count):
            line = jnp.broadcast_to(cw[tile, s, pl.ds(g * UNIT + i, 1), :], (band, 2 * cap))
            mix[i * band : (i + 1) * band, :] = line.astype(jnp.bfloat16) * lines
        at = pl.multiple_of((tile * col_units + g) * unit, unit)
        acc[pl.ds(at, unit * count), :] += jnp.dot(
            mix[pl.ds(0, unit * count), :],
            x_in[tile, pl.ds(pl.multiple_of(2 * s * cap, 2 * cap), 2 * cap), :],
            preferred_element_type=jnp.float32,
        )

    def add_step(s):
        count = span_units // over_units

        def one(i, none):
            contract(s, i // count, i % count * over_units, over_units)
            return none

        lax.fori_loop(0, 2 * count, one, 0)

    take(last, (1 - mine,))
    add_step(last)

    def middle_steps(s, none):
        take(s, (0, 1))
        add_step(s)
        return none

    lax.fori_loop(0, last - 1, middle_steps, 0)
    final = last - 1
    take(final, (0, 1))

    def h_copy(side, u):
        return pltpu.make_async_remote_copy(
            src_ref=h_out.at[side, u],
            dst_ref=h_in.at[1 - side, u],
            send_sem=h_ss.at[side, u],
            recv_sem=h_rs.at[1 - side, u],
            device_id=((left, right)[side], mm),
            device_id_type=MESH,
        )

    def d_copy(side):
        return pltpu.make_async_remote_copy(
            src_ref=d_out.at[side],
            dst_ref=d_in.at[1 - side],
            send_sem=d_ss.at[side],
            recv_sem=d_rs.at[1 - side],
            device_id=((left, right)[side], mm),
            device_id_type=MESH,
        )

    def y_copy(slot, to):
        return pltpu.make_async_remote_copy(
            src_ref=y_out.at[slot],
            dst_ref=t1.at[to, mine],
            send_sem=y_ss.at[slot],
            recv_sem=y_rs.at[slot],
            device_id=(mate, mm),
            device_id_type=MESH,
        )

    def m_copy(side, cg, h):
        start = 0 if side == 0 else band - REACH
        return pltpu.make_async_remote_copy(
            src_ref=t1.at[cg, h, :, pl.ds(start, REACH), :],
            dst_ref=m_in.at[1 - side, cg, h],
            send_sem=m_ss.at[side, cg, h],
            recv_sem=m_rs.at[1 - side, cg, h],
            device_id=(me, (up, down)[side]),
            device_id_type=MESH,
        )

    def m_start(cg, h):
        for side in range(2):
            @pl.when(has_map[side])
            def _(side=side):
                m_copy(side, cg, h).start()

    def dm_copy(side):
        return pltpu.make_async_remote_copy(
            src_ref=d_own,
            dst_ref=dm_in.at[1 - side],
            send_sem=dm_ss.at[side],
            recv_sem=dm_rs.at[1 - side],
            device_id=(me, (up, down)[side]),
            device_id_type=MESH,
        )

    for side in range(2):
        @pl.when(jnp.logical_not(has_map[side]))
        def _(side=side):
            dm_in[side] = jnp.zeros((cols, band), jnp.float32)
            m_in[side] = jnp.zeros(m_in.shape[1:], jnp.bfloat16)

    block = (UNIT, band, part)

    def rounded(u):
        at = pl.multiple_of(u * unit, unit)
        return acc[pl.ds(at, unit), :].astype(jnp.bfloat16).reshape(block)

    for u in range(over_units):
        for side in range(2):
            g = u if side == 0 else col_units + over_units + u
            contract(final, side, g, 1)
            h_out[side, u] = rounded(side * col_units + g)

            @pl.when(has_dp[side])
            def _(side=side, u=u):
                h_copy(side, u).start()

    for m in range(spare):
        n = col_units + m - mine * spare
        contract(final, 0, n + over_units, 1)
        contract(final, 1, n - spare, 1)
        y_out[m] = rounded(n + over_units)
        y_copy(m, m + mine * over_units).start()

    for m in range(spare):
        n = over_units + m + mine * spare
        contract(final, 0, n + over_units, 1)
        contract(final, 1, n - spare, 1)
        t1[m + (1 - mine) * over_units, mine] = rounded(n + over_units)
        m_start(m + (1 - mine) * over_units, mine)

    ends = 2 * col_units - over_units
    for e in range(over_units):
        contract(final, 0, e + over_units, 1)
        contract(final, 1, ends + e - spare, 1)
        if e >= spare:
            contract(final, 1, e - spare, 1)
            contract(final, 0, ends + e + over_units, 1)

    totals = []
    for tile in range(2):
        total = jnp.zeros((span, band), jnp.float32)
        for s in range(pairs):
            total += lax.dot_general(
                cw[tile, s].astype(jnp.bfloat16), rm[tile, s], NT, preferred_element_type=jnp.float32
            )
        totals.append(total)
    d_out[0] = totals[0][:REACH]
    d_out[1] = totals[1][REACH + cols :]
    d_own[...] = jnp.where(
        mine == 0, totals[0][REACH : REACH + cols], totals[1][REACH : REACH + cols]
    )
    d_own[pl.ds(pl.multiple_of((1 - mine) * (cols - REACH), 8), REACH), :] += jnp.where(
        mine == 0, totals[1][:REACH], totals[0][REACH + cols :]
    )
    for side in range(2):
        @pl.when(has_dp[side])
        def _(side=side):
            d_copy(side).start()

    for e in range(over_units):
        for side in range(2):
            @pl.when(has_dp[side])
            def _(side=side, e=e):
                h_copy(1 - side, e).wait_recv()
                at = (over_units + e if side == 0 else over_units + ends + e) * unit
                acc[pl.ds(at, unit), :] += h_in[side, e].reshape(unit, part).astype(jnp.float32)

        y_out[spare + e] = rounded(over_units + e + (1 - mine) * ends)
        y_copy(spare + e, e + (1 - mine) * spare).start()
        t1[e + mine * spare, mine] = rounded(over_units + e + mine * ends)
        m_start(e + mine * spare, mine)

    for side in range(2):
        @pl.when(has_dp[side])
        def _(side=side):
            d_copy(1 - side).wait_recv()

        @pl.when(has_dp[side] & (mine == side))
        def _(side=side):
            base = 0 if side == 0 else cols - REACH
            d_own[pl.ds(base, REACH), :] += d_in[side]

    for side in range(2):
        @pl.when(has_map[side])
        def _(side=side):
            dm_copy(side).start()

    gap = iota((band, band + 2 * REACH), 0) + REACH - iota((band, band + 2 * REACH), 1)
    taps = weight(gap.astype(jnp.float32)).astype(jnp.bfloat16)

    def finish(u, h):
        for side in range(2):
            @pl.when(has_map[side])
            def _(side=side):
                m_copy(1 - side, u, h).wait_recv()

        for i in range(0, UNIT, 2):
            ext = jnp.concatenate(
                [
                    jnp.concatenate([m_in[0, u, h, i + k], t1[u, h, i + k], m_in[1, u, h, i + k]], axis=0)
                    for k in range(2)
                ],
                axis=1,
            )
            got = jnp.dot(taps, ext, preferred_element_type=jnp.float32).astype(jnp.bfloat16)
            for k in range(2):
                num_ref[u * UNIT + i + k, :, pl.ds(pl.multiple_of(h * part, part), part)] = got[
                    :, k * part : (k + 1) * part
                ]

    for m in range(spare):
        y_copy(m, 0).wait_recv()
        m_start(m + (1 - mine) * over_units, 1 - mine)
    for m in range(spare):
        finish(m + (1 - mine) * over_units, mine)
    for side in range(2):
        @pl.when(has_map[side])
        def _(side=side):
            dm_copy(1 - side).wait_recv()

    den = jnp.zeros((cols, band), jnp.float32)
    apart = (iota((band, band), 0) - iota((band, band), 1)).astype(jnp.float32)
    for p, counts in enumerate((dm_in[0], d_own[...], dm_in[1])):
        row_taps = weight(apart + float((1 - p) * band)).astype(jnp.bfloat16).astype(jnp.float32)
        den += lax.dot_general(
            counts, row_taps, NT, precision=lax.Precision.HIGHEST, preferred_element_type=jnp.float32
        )
    scale_ref[...] = 0.9 / (den + 1.0)
    for e in range(over_units):
        finish(e + mine * spare, mine)
    for m in range(spare):
        finish(m + (1 - mine) * over_units, 1 - mine)
    for e in range(over_units):
        y_copy(spare + e, 0).wait_recv()
        m_start(e + mine * spare, 1 - mine)
    for e in range(over_units):
        finish(e + mine * spare, 1 - mine)

    def sent(i, none):
        s, tile = i // 2, i % 2
        for to in range(2):
            @pl.when((s < last) | (mine != to))
            def _(to=to):
                k_copy(s, tile, to, mine).wait_send()
                x_copy(s, tile, to, mine).wait_send()

        return none

    lax.fori_loop(0, 2 * pairs, sent, 0)
    for u in range(col_units):
        y_copy(u, 0).wait_send()
    for side in range(2):
        @pl.when(has_dp[side])
        def _(side=side):
            d_copy(side).wait_send()
            for u in range(over_units):
                h_copy(side, u).wait_send()

        @pl.when(has_map[side])
        def _(side=side):
            dm_copy(side).wait_send()
            for u in range(col_units):
                for h in range(HALVES):
                    m_copy(side, u, h).wait_send()


def on_device(embeddings, winners, codebook):
    cols, band, width = codebook.shape
    n_dp = lax.axis_size("dp")
    n_map = lax.axis_size("map")
    rows = embeddings.shape[0]
    cap = max(2, 2 * rows // (n_dp * n_map))
    slots = n_dp * cap
    part = width // HALVES
    pairs = n_dp // 2
    units = cols // UNIT
    past = REACH // UNIT
    unit = UNIT * band
    span = cols + 2 * REACH
    bf16, f32 = jnp.bfloat16, jnp.float32
    vmem = pl.BlockSpec(memory_space=pltpu.VMEM)
    dma = pltpu.SemaphoreType.DMA
    num, scale = pl.pallas_call(
        functools.partial(exchange_kernel, (n_dp, n_map, cap, cols, band, rows, width)),
        out_shape=(
            jax.ShapeDtypeStruct((cols, band, width), bf16),
            jax.ShapeDtypeStruct((cols, band), f32),
        ),
        in_specs=[pl.BlockSpec(memory_space=pl.ANY), vmem],
        out_specs=(vmem, vmem),
        scratch_shapes=[
            pltpu.VMEM((rows, width), bf16),
            pltpu.VMEM((n_dp, rows), jnp.int32),
            pltpu.VMEM((1, rows), f32),
            pltpu.VMEM((pairs, HALVES, 2, cap, part), bf16),
            pltpu.VMEM((2, slots, part), bf16),
            pltpu.VMEM((pairs, 2, 8, cap), f32),
            pltpu.VMEM((pairs, 2, 2, 8, cap), f32),
            pltpu.VMEM((2, pairs, span, 2 * cap), f32),
            pltpu.VMEM((2, pairs, band, 2 * cap), bf16),
            pltpu.VMEM((REACH * band, 2 * cap), bf16),
            pltpu.VMEM((2 * (units + past) * unit, part), f32),
            pltpu.VMEM((2, past, UNIT, band, part), bf16),
            pltpu.VMEM((2, past, UNIT, band, part), bf16),
            pltpu.VMEM((2, REACH, band), f32),
            pltpu.VMEM((2, REACH, band), f32),
            pltpu.VMEM((cols, band), f32),
            pltpu.VMEM((units, UNIT, band, part), bf16),
            pltpu.VMEM((units, HALVES, UNIT, band, part), bf16),
            pltpu.VMEM((2, units, HALVES, UNIT, REACH, part), bf16),
            pltpu.VMEM((2, cols, band), f32),
            dma,
            dma((pairs, 2, 2)), dma((pairs, 2, 2)), dma((pairs, 2, 2)), dma((pairs, 2, 2)),
            dma((2, past)), dma((2, past)), dma((2,)), dma((2,)), dma((units,)), dma((units,)),
            dma((2, units, HALVES)), dma((2, units, HALVES)), dma((2,)), dma((2,)),
        ],
        compiler_params=pltpu.CompilerParams(
            collective_id=0, has_side_effects=True, vmem_limit_bytes=56 * 1024 * 1024
        ),
        cost_estimate=pl.CostEstimate(
            flops=2 * width * slots * (rows + span * band),
            bytes_accessed=2 * width * (rows + cols * (band + 2 * REACH)),
            transcendentals=span * slots,
        ),
    )(embeddings, winners.reshape(1, rows))

    updated = 0.1 * codebook + (num.astype(f32) + codebook) * scale[:, :, None]
    return updated, updated.astype(bf16)


def solution(mesh):
    placed = (P("dp", None), P("dp"), P("dp", "map", None))
    return jax.shard_map(
        on_device,
        mesh=mesh,
        in_specs=placed,
        out_specs=(P("dp", "map", None), P("dp", "map", None)),
        check_vma=False,
    )
```

```python
import functools

import jax
import jax.numpy as jnp
from jax import lax
from jax.experimental import pallas as pl
from jax.experimental.pallas import tpu as pltpu
from jax.sharding import PartitionSpec as P

REACH = 16
SIGMA = float(REACH) / 2.0
HALVES = 2
UNIT = REACH // 2
MESH = pl.DeviceIdType.MESH
NT = (((1,), (1,)), ((), ()))


def iota(shape, dim):
    return lax.broadcasted_iota(jnp.int32, shape, dim)


def over(values, size):
    if size & (size - 1) == 0:
        return lax.shift_right_logical(values, jnp.int32(size.bit_length() - 1))
    return values // size


def weight(gap):
    apart = gap / SIGMA
    return jnp.where(jnp.abs(gap) <= REACH, jnp.exp(-0.5 * apart * apart) / SIGMA, 0.0)


def exchange_kernel(
    dims, emb_hbm, win_ref, num_ref, scale_ref,
    emb, rank, keys, x_out, x_in, k_out, k_in, cw, rm, mix, acc, h_out, h_in, d_out, d_in, d_own, y_out, t1, m_in,
    dm_in, e_sem, x_ss, x_rs, k_ss, k_rs, h_ss, h_rs, d_ss, d_rs, y_ss, y_rs, m_ss, m_rs, dm_ss, dm_rs,
):
    n_dp, n_map, cap, cols, band, rows, width = dims
    part = width // HALVES
    unit = UNIT * band
    over_units = REACH // UNIT
    col_units = cols // UNIT
    spare = col_units - over_units
    span_units = col_units + 2 * over_units
    pairs = n_dp // 2
    me = lax.axis_index("dp")
    mm = lax.axis_index("map")
    pair, mine = me // 2, me % 2
    mate = 2 * pair + 1 - mine
    left, right = lax.rem(me + n_dp - 2, n_dp), lax.rem(me + 2, n_dp)
    up, down = lax.rem(mm + n_map - 1, n_map), lax.rem(mm + 1, n_map)
    has_dp = (pair > 0, pair < pairs - 1)
    has_map = (mm > 0, mm < n_map - 1)

    fetch = pltpu.make_async_copy(emb_hbm, emb, e_sem)
    fetch.start()
    barrier = pltpu.get_barrier_semaphore()
    for k in range(1, n_dp):
        pl.semaphore_signal(
            barrier, inc=1, device_id=(lax.rem(me + k, n_dp), mm), device_id_type=MESH
        )
    for other in (up, down):
        pl.semaphore_signal(barrier, inc=1, device_id=(me, other), device_id_type=MESH)

    win = win_ref[...]
    column = over(win, band * n_map)
    row_of = win - column * (band * n_map) - mm * band
    target = over(column, cols)
    local = column - target * cols
    inside = (row_of >= 0) & (row_of < band)
    target = jnp.where(inside, target, -1)
    step = 256
    upper = jnp.where(iota((step, step), 0) <= iota((step, step), 1), 1.0, 0.0).astype(jnp.bfloat16)
    hits = jnp.where(target == iota((n_dp, rows), 0), 1.0, 0.0)
    carry = jnp.zeros((n_dp, 1), jnp.float32)
    for j in range(rows // step):
        hit = hits[:, j * step : (j + 1) * step]
        count = jnp.dot(hit.astype(jnp.bfloat16), upper, preferred_element_type=jnp.float32) + carry
        carry = count[:, step - 1 : step]
        rank[:, j * step : (j + 1) * step] = jnp.where(hit > 0.0, count - 1.0, -1.0)

    high = cap // 16
    slot = jnp.max(rank[...], axis=0, keepdims=True).astype(jnp.int32)
    where_high = jnp.where(slot >= 0, target * high + over(slot, 16), -1)
    tall = jnp.where(iota((n_dp * high, rows), 0) == where_high, 1.0, 0.0).astype(jnp.bfloat16)
    low = iota((16, rows), 0) == slot % 16
    tags = jnp.concatenate(
        [jnp.where(low, of.astype(jnp.float32), 0.0) for of in (local, row_of, jnp.ones_like(local))], axis=0
    ).astype(jnp.bfloat16)
    table = lax.dot_general(tall, tags, NT, preferred_element_type=jnp.float32)
    lane = iota((48, cap), 0)
    spread = jnp.where(
        lane % 16 == iota((48, cap), 1) % 16, jnp.where(lane < 16, float(band), 1.0), 0.0
    ).astype(jnp.bfloat16)
    table = jnp.dot(table.astype(jnp.bfloat16), spread, preferred_element_type=jnp.float32)
    table = jnp.where(iota((n_dp * high, cap), 0) % high == over(iota((n_dp * high, cap), 1), 16), table, 0.0)
    join = jnp.where(iota((n_dp, n_dp * high), 0) == over(iota((n_dp, n_dp * high), 1), high), 1.0, 0.0)
    keys[...] = jnp.dot(
        join, table, precision=lax.Precision.HIGHEST, preferred_element_type=jnp.float32
    )

    fetch.wait()
    pl.semaphore_wait(barrier, n_dp + 1)

    def plane(s):
        half = (s + 1) // 2
        return lax.rem(pair + pairs // 2 + half * (1 - 2 * (s % 2)), pairs)

    def place(s, sender):
        return pl.ds(pl.multiple_of((2 * s + sender) * cap, cap), cap)

    def x_copy(s, tile, to, sender):
        return pltpu.make_async_remote_copy(
            src_ref=x_out.at[s, to, tile],
            dst_ref=x_in.at[tile, place(s, sender), :],
            send_sem=x_ss.at[s, to, tile],
            recv_sem=x_rs.at[s, sender, tile],
            device_id=(2 * plane(s) + to, mm),
            device_id_type=MESH,
        )

    def k_copy(s, tile, to, sender):
        return pltpu.make_async_remote_copy(
            src_ref=k_out.at[s, tile],
            dst_ref=k_in.at[s, sender, tile],
            send_sem=k_ss.at[s, to, tile],
            recv_sem=k_rs.at[s, sender, tile],
            device_id=(2 * plane(s) + to, mm),
            device_id_type=MESH,
        )

    last = pairs - 1

    def send_keys(i, none):
        s, tile = i // 2, i % 2
        k_out[s, tile] = jnp.broadcast_to(keys[pl.ds(2 * plane(s) + tile, 1), :], (8, cap))

        @pl.when(s < last)
        def _():
            for to in range(2):
                k_copy(s, tile, to, mine).start()

        @pl.when(s == last)
        def _():
            k_copy(s, tile, 1 - mine, mine).start()
            k_in[s, mine, tile] = k_out[s, tile]

        return none

    lax.fori_loop(0, 2 * pairs, send_keys, 0)
    piece = rows // 4
    slot_of = iota((cap, piece), 0).astype(jnp.float32).astype(jnp.bfloat16)
    one, nought = jnp.bfloat16(1.0), jnp.bfloat16(0.0)

    def send(s, none):
        packed = jnp.zeros((2 * cap, width), jnp.float32)
        for q in range(4):
            chosen = jnp.concatenate(
                [
                    jnp.where(
                        rank[pl.ds(2 * plane(s) + tile, 1), q * piece : (q + 1) * piece].astype(jnp.bfloat16)
                        == slot_of,
                        one,
                        nought,
                    )
                    for tile in range(2)
                ],
                axis=0,
            )
            packed += jnp.dot(
                chosen, emb[q * piece : (q + 1) * piece, :], preferred_element_type=jnp.float32
            )
        packed = packed.astype(jnp.bfloat16)
        for tile in range(2):
            for h in range(HALVES):
                x_out[s, h, tile] = packed[tile * cap : (tile + 1) * cap, h * part : (h + 1) * part]

        @pl.when(s < last)
        def _():
            for tile in range(2):
                for to in range(2):
                    x_copy(s, tile, to, mine).start()

        @pl.when(s == last)
        def _():
            for tile in range(2):
                x_copy(s, tile, 1 - mine, mine).start()
                x_in[tile, place(s, mine), :] = x_out[s, mine, tile]

        return none

    lax.fori_loop(0, pairs, send, 0)
    acc[...] = jnp.zeros_like(acc)

    span = cols + 2 * REACH

    def take(s, senders):
        for sender in senders:
            for tile in range(2):
                k_copy(s, tile, 1 - mine, sender).wait_recv()
                x_copy(s, tile, 1 - mine, sender).wait_recv()
        for sender in range(2):
            for tile in range(2):
                key = k_in[s, sender, tile][0:1, :].astype(jnp.int32) - 1
                at = over(key, band)
                gap = (iota((span, cap), 0) - REACH - at).astype(jnp.float32)
                lanes = slice(sender * cap, (sender + 1) * cap)
                cw[tile, s, :, lanes] = weight(gap)
                rm[tile, s, :, lanes] = jnp.where(
                    iota((band, cap), 0) == key - at * band, 1.0, 0.0
                ).astype(jnp.bfloat16)

    def contract(s, tile, g, count):
        lines = rm[tile, s]
        for i in range(UNIT * count):
            line = jnp.broadcast_to(cw[tile, s, pl.ds(g * UNIT + i, 1), :], (band, 2 * cap))
            mix[i * band : (i + 1) * band, :] = line.astype(jnp.bfloat16) * lines
        at = pl.multiple_of((tile * col_units + g) * unit, unit)
        acc[pl.ds(at, unit * count), :] += jnp.dot(
            mix[pl.ds(0, unit * count), :],
            x_in[tile, pl.ds(pl.multiple_of(2 * s * cap, 2 * cap), 2 * cap), :],
            preferred_element_type=jnp.float32,
        )

    def add_step(s):
        count = span_units // over_units

        def one(i, none):
            contract(s, i // count, i % count * over_units, over_units)
            return none

        lax.fori_loop(0, 2 * count, one, 0)

    take(last, (1 - mine,))
    add_step(last)

    def middle_steps(s, none):
        take(s, (0, 1))
        add_step(s)
        return none

    lax.fori_loop(0, last - 1, middle_steps, 0)
    final = last - 1
    take(final, (0, 1))

    def h_copy(side, u):
        return pltpu.make_async_remote_copy(
            src_ref=h_out.at[side, u],
            dst_ref=h_in.at[1 - side, u],
            send_sem=h_ss.at[side, u],
            recv_sem=h_rs.at[1 - side, u],
            device_id=((left, right)[side], mm),
            device_id_type=MESH,
        )

    def d_copy(side):
        return pltpu.make_async_remote_copy(
            src_ref=d_out.at[side],
            dst_ref=d_in.at[1 - side],
            send_sem=d_ss.at[side],
            recv_sem=d_rs.at[1 - side],
            device_id=((left, right)[side], mm),
            device_id_type=MESH,
        )

    def y_copy(slot, to):
        return pltpu.make_async_remote_copy(
            src_ref=y_out.at[slot],
            dst_ref=t1.at[to, mine],
            send_sem=y_ss.at[slot],
            recv_sem=y_rs.at[slot],
            device_id=(mate, mm),
            device_id_type=MESH,
        )

    def m_copy(side, cg, h):
        start = 0 if side == 0 else band - REACH
        return pltpu.make_async_remote_copy(
            src_ref=t1.at[cg, h, :, pl.ds(start, REACH), :],
            dst_ref=m_in.at[1 - side, cg, h],
            send_sem=m_ss.at[side, cg, h],
            recv_sem=m_rs.at[1 - side, cg, h],
            device_id=(me, (up, down)[side]),
            device_id_type=MESH,
        )

    def m_start(cg, h):
        for side in range(2):
            @pl.when(has_map[side])
            def _(side=side):
                m_copy(side, cg, h).start()

    def dm_copy(side):
        return pltpu.make_async_remote_copy(
            src_ref=d_own,
            dst_ref=dm_in.at[1 - side],
            send_sem=dm_ss.at[side],
            recv_sem=dm_rs.at[1 - side],
            device_id=(me, (up, down)[side]),
            device_id_type=MESH,
        )

    for side in range(2):
        @pl.when(jnp.logical_not(has_map[side]))
        def _(side=side):
            dm_in[side] = jnp.zeros((cols, band), jnp.float32)
            m_in[side] = jnp.zeros(m_in.shape[1:], jnp.bfloat16)

    block = (UNIT, band, part)

    def rounded(u):
        at = pl.multiple_of(u * unit, unit)
        return acc[pl.ds(at, unit), :].astype(jnp.bfloat16).reshape(block)

    for u in range(over_units):
        for side in range(2):
            g = u if side == 0 else col_units + over_units + u
            contract(final, side, g, 1)
            h_out[side, u] = rounded(side * col_units + g)

            @pl.when(has_dp[side])
            def _(side=side, u=u):
                h_copy(side, u).start()

    for m in range(spare):
        n = col_units + m - mine * spare
        contract(final, 0, n + over_units, 1)
        contract(final, 1, n - spare, 1)
        y_out[m] = rounded(n + over_units)
        y_copy(m, m + mine * over_units).start()

    for m in range(spare):
        n = over_units + m + mine * spare
        contract(final, 0, n + over_units, 1)
        contract(final, 1, n - spare, 1)
        t1[m + (1 - mine) * over_units, mine] = rounded(n + over_units)
        m_start(m + (1 - mine) * over_units, mine)

    ends = 2 * col_units - over_units
    for e in range(over_units):
        contract(final, 0, e + over_units, 1)
        contract(final, 1, ends + e - spare, 1)
        if e >= spare:
            contract(final, 1, e - spare, 1)
            contract(final, 0, ends + e + over_units, 1)

    totals = []
    for tile in range(2):
        total = jnp.zeros((span, band), jnp.float32)
        for s in range(pairs):
            total += lax.dot_general(
                cw[tile, s].astype(jnp.bfloat16), rm[tile, s], NT, preferred_element_type=jnp.float32
            )
        totals.append(total)
    d_out[0] = totals[0][:REACH]
    d_out[1] = totals[1][REACH + cols :]
    d_own[...] = jnp.where(
        mine == 0, totals[0][REACH : REACH + cols], totals[1][REACH : REACH + cols]
    )
    d_own[pl.ds(pl.multiple_of((1 - mine) * (cols - REACH), 8), REACH), :] += jnp.where(
        mine == 0, totals[1][:REACH], totals[0][REACH + cols :]
    )
    for side in range(2):
        @pl.when(has_dp[side])
        def _(side=side):
            d_copy(side).start()

    for e in range(over_units):
        for side in range(2):
            @pl.when(has_dp[side])
            def _(side=side, e=e):
                h_copy(1 - side, e).wait_recv()
                at = (over_units + e if side == 0 else over_units + ends + e) * unit
                acc[pl.ds(at, unit), :] += h_in[side, e].reshape(unit, part).astype(jnp.float32)

        y_out[spare + e] = rounded(over_units + e + (1 - mine) * ends)
        y_copy(spare + e, e + (1 - mine) * spare).start()
        t1[e + mine * spare, mine] = rounded(over_units + e + mine * ends)
        m_start(e + mine * spare, mine)

    for side in range(2):
        @pl.when(has_dp[side])
        def _(side=side):
            d_copy(1 - side).wait_recv()

        @pl.when(has_dp[side] & (mine == side))
        def _(side=side):
            base = 0 if side == 0 else cols - REACH
            d_own[pl.ds(base, REACH), :] += d_in[side]

    for side in range(2):
        @pl.when(has_map[side])
        def _(side=side):
            dm_copy(side).start()

    gap = iota((band, band + 2 * REACH), 0) + REACH - iota((band, band + 2 * REACH), 1)
    taps = weight(gap.astype(jnp.float32)).astype(jnp.bfloat16)

    def finish(u, h):
        for side in range(2):
            @pl.when(has_map[side])
            def _(side=side):
                m_copy(1 - side, u, h).wait_recv()

        for i in range(0, UNIT, 2):
            ext = jnp.concatenate(
                [
                    jnp.concatenate([m_in[0, u, h, i + k], t1[u, h, i + k], m_in[1, u, h, i + k]], axis=0)
                    for k in range(2)
                ],
                axis=1,
            )
            got = jnp.dot(taps, ext, preferred_element_type=jnp.float32).astype(jnp.bfloat16)
            for k in range(2):
                num_ref[u * UNIT + i + k, :, pl.ds(pl.multiple_of(h * part, part), part)] = got[
                    :, k * part : (k + 1) * part
                ]

    for m in range(spare):
        y_copy(m, 0).wait_recv()
        m_start(m + (1 - mine) * over_units, 1 - mine)
    for m in range(spare):
        finish(m + (1 - mine) * over_units, mine)
    for side in range(2):
        @pl.when(has_map[side])
        def _(side=side):
            dm_copy(1 - side).wait_recv()

    den = jnp.zeros((cols, band), jnp.float32)
    apart = (iota((band, band), 0) - iota((band, band), 1)).astype(jnp.float32)
    for p, counts in enumerate((dm_in[0], d_own[...], dm_in[1])):
        row_taps = weight(apart + float((1 - p) * band)).astype(jnp.bfloat16).astype(jnp.float32)
        den += lax.dot_general(
            counts, row_taps, NT, precision=lax.Precision.HIGHEST, preferred_element_type=jnp.float32
        )
    scale_ref[...] = 0.9 / (den + 1.0)
    for e in range(over_units):
        finish(e + mine * spare, mine)
    for m in range(spare):
        finish(m + (1 - mine) * over_units, 1 - mine)
    for e in range(over_units):
        y_copy(spare + e, 0).wait_recv()
        m_start(e + mine * spare, 1 - mine)
    for e in range(over_units):
        finish(e + mine * spare, 1 - mine)

    def sent(i, none):
        s, tile = i // 2, i % 2
        for to in range(2):
            @pl.when((s < last) | (mine != to))
            def _(to=to):
                k_copy(s, tile, to, mine).wait_send()
                x_copy(s, tile, to, mine).wait_send()

        return none

    lax.fori_loop(0, 2 * pairs, sent, 0)
    for u in range(col_units):
        y_copy(u, 0).wait_send()
    for side in range(2):
        @pl.when(has_dp[side])
        def _(side=side):
            d_copy(side).wait_send()
            for u in range(over_units):
                h_copy(side, u).wait_send()

        @pl.when(has_map[side])
        def _(side=side):
            dm_copy(side).wait_send()
            for u in range(col_units):
                for h in range(HALVES):
                    m_copy(side, u, h).wait_send()


def on_device(embeddings, winners, codebook):
    cols, band, width = codebook.shape
    n_dp = lax.axis_size("dp")
    n_map = lax.axis_size("map")
    rows = embeddings.shape[0]
    cap = max(2, 2 * rows // (n_dp * n_map))
    slots = n_dp * cap
    part = width // HALVES
    pairs = n_dp // 2
    units = cols // UNIT
    past = REACH // UNIT
    unit = UNIT * band
    span = cols + 2 * REACH
    bf16, f32 = jnp.bfloat16, jnp.float32
    vmem = pl.BlockSpec(memory_space=pltpu.VMEM)
    dma = pltpu.SemaphoreType.DMA
    num, scale = pl.pallas_call(
        functools.partial(exchange_kernel, (n_dp, n_map, cap, cols, band, rows, width)),
        out_shape=(
            jax.ShapeDtypeStruct((cols, band, width), bf16),
            jax.ShapeDtypeStruct((cols, band), f32),
        ),
        in_specs=[pl.BlockSpec(memory_space=pl.ANY), vmem],
        out_specs=(vmem, vmem),
        scratch_shapes=[
            pltpu.VMEM((rows, width), bf16),
            pltpu.VMEM((n_dp, rows), f32),
            pltpu.VMEM((n_dp, cap), f32),
            pltpu.VMEM((pairs, HALVES, 2, cap, part), bf16),
            pltpu.VMEM((2, slots, part), bf16),
            pltpu.VMEM((pairs, 2, 8, cap), f32),
            pltpu.VMEM((pairs, 2, 2, 8, cap), f32),
            pltpu.VMEM((2, pairs, span, 2 * cap), f32),
            pltpu.VMEM((2, pairs, band, 2 * cap), bf16),
            pltpu.VMEM((REACH * band, 2 * cap), bf16),
            pltpu.VMEM((2 * (units + past) * unit, part), f32),
            pltpu.VMEM((2, past, UNIT, band, part), bf16),
            pltpu.VMEM((2, past, UNIT, band, part), bf16),
            pltpu.VMEM((2, REACH, band), f32),
            pltpu.VMEM((2, REACH, band), f32),
            pltpu.VMEM((cols, band), f32),
            pltpu.VMEM((units, UNIT, band, part), bf16),
            pltpu.VMEM((units, HALVES, UNIT, band, part), bf16),
            pltpu.VMEM((2, units, HALVES, UNIT, REACH, part), bf16),
            pltpu.VMEM((2, cols, band), f32),
            dma,
            dma((pairs, 2, 2)), dma((pairs, 2, 2)), dma((pairs, 2, 2)), dma((pairs, 2, 2)),
            dma((2, past)), dma((2, past)), dma((2,)), dma((2,)), dma((units,)), dma((units,)),
            dma((2, units, HALVES)), dma((2, units, HALVES)), dma((2,)), dma((2,)),
        ],
        compiler_params=pltpu.CompilerParams(
            collective_id=0, has_side_effects=True, vmem_limit_bytes=56 * 1024 * 1024
        ),
        cost_estimate=pl.CostEstimate(
            flops=2 * width * slots * (rows + span * band),
            bytes_accessed=2 * width * (rows + cols * (band + 2 * REACH)),
            transcendentals=span * slots,
        ),
    )(embeddings, winners.reshape(1, rows))

    updated = 0.1 * codebook + (num.astype(f32) + codebook) * scale[:, :, None]
    return updated, updated.astype(bf16)


def solution(mesh):
    placed = (P("dp", None), P("dp"), P("dp", "map", None))
    return jax.shard_map(
        on_device,
        mesh=mesh,
        in_specs=placed,
        out_specs=(P("dp", "map", None), P("dp", "map", None)),
        check_vma=False,
    )
```

```python
import functools

import jax
import jax.numpy as jnp
from jax import lax
from jax.experimental import pallas as pl
from jax.experimental.pallas import tpu as pltpu
from jax.sharding import PartitionSpec as P

REACH = 16
SIGMA = float(REACH) / 2.0
HALVES = 2
UNIT = REACH // 2
MESH = pl.DeviceIdType.MESH
NT = (((1,), (1,)), ((), ()))


def iota(shape, dim):
    return lax.broadcasted_iota(jnp.int32, shape, dim)


def over(values, size):
    if size & (size - 1) == 0:
        return lax.shift_right_logical(values, jnp.int32(size.bit_length() - 1))
    return values // size


def weight(gap):
    apart = gap / SIGMA
    return jnp.where(jnp.abs(gap) <= REACH, jnp.exp(-0.5 * apart * apart) / SIGMA, 0.0)


def exchange_kernel(
    dims, emb_hbm, win_ref, num_ref, scale_ref,
    emb, rank, keys, x_out, x_in, k_out, k_in, cw, rm, mix, acc, h_out, h_in, d_out, d_in, d_own, y_out, t1, m_in,
    dm_in, e_sem, x_ss, x_rs, k_ss, k_rs, h_ss, h_rs, d_ss, d_rs, y_ss, y_rs, m_ss, m_rs, dm_ss, dm_rs,
):
    n_dp, n_map, cap, cols, band, rows, width = dims
    part = width // HALVES
    unit = UNIT * band
    over_units = REACH // UNIT
    col_units = cols // UNIT
    spare = col_units - over_units
    span_units = col_units + 2 * over_units
    pairs = n_dp // 2
    me = lax.axis_index("dp")
    mm = lax.axis_index("map")
    pair, mine = me // 2, me % 2
    mate = 2 * pair + 1 - mine
    left, right = lax.rem(me + n_dp - 2, n_dp), lax.rem(me + 2, n_dp)
    up, down = lax.rem(mm + n_map - 1, n_map), lax.rem(mm + 1, n_map)
    has_dp = (pair > 0, pair < pairs - 1)
    has_map = (mm > 0, mm < n_map - 1)

    fetch = pltpu.make_async_copy(emb_hbm, emb, e_sem)
    fetch.start()
    barrier = pltpu.get_barrier_semaphore()
    for k in range(1, n_dp):
        pl.semaphore_signal(
            barrier, inc=1, device_id=(lax.rem(me + k, n_dp), mm), device_id_type=MESH
        )
    for other in (up, down):
        pl.semaphore_signal(barrier, inc=1, device_id=(me, other), device_id_type=MESH)

    win = win_ref[...]
    column = over(win, band * n_map)
    row_of = win - column * (band * n_map) - mm * band
    target = over(column, cols)
    local = column - target * cols
    inside = (row_of >= 0) & (row_of < band)
    target = jnp.where(inside, target, -1)
    step = 256
    upper = jnp.where(iota((step, step), 0) <= iota((step, step), 1), 1.0, 0.0).astype(jnp.bfloat16)
    hits = jnp.where(target == iota((n_dp, rows), 0), 1.0, 0.0)
    carry = jnp.zeros((n_dp, 1), jnp.float32)
    for j in range(rows // step):
        hit = hits[:, j * step : (j + 1) * step]
        count = jnp.dot(hit.astype(jnp.bfloat16), upper, preferred_element_type=jnp.float32) + carry
        carry = count[:, step - 1 : step]
        rank[:, j * step : (j + 1) * step] = jnp.where(hit > 0.0, count - 1.0, -1.0)

    fetch.wait()
    pl.semaphore_wait(barrier, n_dp + 1)

    def plane(s):
        half = (s + 1) // 2
        return lax.rem(pair + pairs // 2 + half * (1 - 2 * (s % 2)), pairs)

    def place(s, sender):
        return pl.ds(pl.multiple_of((2 * s + sender) * cap, cap), cap)

    def x_copy(s, tile, to, sender):
        return pltpu.make_async_remote_copy(
            src_ref=x_out.at[s, to, tile],
            dst_ref=x_in.at[tile, place(s, sender), :],
            send_sem=x_ss.at[s, to, tile],
            recv_sem=x_rs.at[s, sender, tile],
            device_id=(2 * plane(s) + to, mm),
            device_id_type=MESH,
        )

    def k_copy(s, tile, to, sender):
        return pltpu.make_async_remote_copy(
            src_ref=k_out.at[s, tile],
            dst_ref=k_in.at[s, sender, tile],
            send_sem=k_ss.at[s, to, tile],
            recv_sem=k_rs.at[s, sender, tile],
            device_id=(2 * plane(s) + to, mm),
            device_id_type=MESH,
        )

    last = pairs - 1

    piece = rows // 4
    slot_of = iota((cap, piece), 0).astype(jnp.float32).astype(jnp.bfloat16)
    one, nought = jnp.bfloat16(1.0), jnp.bfloat16(0.0)

    def send(s, none):
        packed = jnp.zeros((2 * cap, width), jnp.float32)
        for q in range(4):
            chosen = jnp.concatenate(
                [
                    jnp.where(
                        rank[pl.ds(2 * plane(s) + tile, 1), q * piece : (q + 1) * piece].astype(jnp.bfloat16)
                        == slot_of,
                        one,
                        nought,
                    )
                    for tile in range(2)
                ],
                axis=0,
            )
            packed += jnp.dot(
                chosen, emb[q * piece : (q + 1) * piece, :], preferred_element_type=jnp.float32
            )
        packed = packed.astype(jnp.bfloat16)
        for tile in range(2):
            for h in range(HALVES):
                x_out[s, h, tile] = packed[tile * cap : (tile + 1) * cap, h * part : (h + 1) * part]

        @pl.when(s < last)
        def _():
            for tile in range(2):
                for to in range(2):
                    x_copy(s, tile, to, mine).start()

        @pl.when(s == last)
        def _():
            for tile in range(2):
                x_copy(s, tile, 1 - mine, mine).start()
                x_in[tile, place(s, mine), :] = x_out[s, mine, tile]

        return none

    lax.fori_loop(0, 1, send, 0)

    high = cap // 16
    slot = jnp.max(rank[...], axis=0, keepdims=True).astype(jnp.int32)
    where_high = jnp.where(slot >= 0, target * high + over(slot, 16), -1)
    tall = jnp.where(iota((n_dp * high, rows), 0) == where_high, 1.0, 0.0).astype(jnp.bfloat16)
    low = iota((16, rows), 0) == slot % 16
    tags = jnp.concatenate(
        [jnp.where(low, of.astype(jnp.float32), 0.0) for of in (local, row_of, jnp.ones_like(local))], axis=0
    ).astype(jnp.bfloat16)
    table = lax.dot_general(tall, tags, NT, preferred_element_type=jnp.float32)
    lane = iota((48, cap), 0)
    spread = jnp.where(
        lane % 16 == iota((48, cap), 1) % 16, jnp.where(lane < 16, float(band), 1.0), 0.0
    ).astype(jnp.bfloat16)
    table = jnp.dot(table.astype(jnp.bfloat16), spread, preferred_element_type=jnp.float32)
    table = jnp.where(iota((n_dp * high, cap), 0) % high == over(iota((n_dp * high, cap), 1), 16), table, 0.0)
    join = jnp.where(iota((n_dp, n_dp * high), 0) == over(iota((n_dp, n_dp * high), 1), high), 1.0, 0.0)
    keys[...] = jnp.dot(
        join, table, precision=lax.Precision.HIGHEST, preferred_element_type=jnp.float32
    )

    def send_keys(i, none):
        s, tile = i // 2, i % 2
        k_out[s, tile] = jnp.broadcast_to(keys[pl.ds(2 * plane(s) + tile, 1), :], (8, cap))

        @pl.when(s < last)
        def _():
            for to in range(2):
                k_copy(s, tile, to, mine).start()

        @pl.when(s == last)
        def _():
            k_copy(s, tile, 1 - mine, mine).start()
            k_in[s, mine, tile] = k_out[s, tile]

        return none

    lax.fori_loop(0, 2 * pairs, send_keys, 0)
    lax.fori_loop(1, pairs, send, 0)
    acc[...] = jnp.zeros_like(acc)

    span = cols + 2 * REACH

    def take(s, senders, tiles=(0, 1)):
        for sender in senders:
            for tile in tiles:
                k_copy(s, tile, 1 - mine, sender).wait_recv()
                x_copy(s, tile, 1 - mine, sender).wait_recv()
        for sender in range(2):
            for tile in tiles:
                key = k_in[s, sender, tile][0:1, :].astype(jnp.int32) - 1
                at = over(key, band)
                gap = (iota((span, cap), 0) - REACH - at).astype(jnp.float32)
                lanes = slice(sender * cap, (sender + 1) * cap)
                cw[tile, s, :, lanes] = weight(gap)
                rm[tile, s, :, lanes] = jnp.where(
                    iota((band, cap), 0) == key - at * band, 1.0, 0.0
                ).astype(jnp.bfloat16)

    def contract(s, tile, g, count):
        lines = rm[tile, s]
        at_mix = tile * REACH * band
        for i in range(UNIT * count):
            line = jnp.broadcast_to(cw[tile, s, pl.ds(g * UNIT + i, 1), :], (band, 2 * cap))
            mix[at_mix + i * band : at_mix + (i + 1) * band, :] = line.astype(jnp.bfloat16) * lines
        at = pl.multiple_of((tile * col_units + g) * unit, unit)
        acc[pl.ds(at, unit * count), :] += jnp.dot(
            mix[at_mix : at_mix + unit * count, :],
            x_in[tile, pl.ds(pl.multiple_of(2 * s * cap, 2 * cap), 2 * cap), :],
            preferred_element_type=jnp.float32,
        )

    def add_step(s):
        count = span_units // over_units

        def one(i, none):
            for tile in range(2):
                contract(s, tile, i * over_units, over_units)
            return none

        lax.fori_loop(0, count, one, 0)

    take(last, (1 - mine,))
    add_step(last)

    def middle_steps(s, none):
        take(s, (0, 1))
        add_step(s)
        return none

    lax.fori_loop(0, last - 1, middle_steps, 0)
    final = last - 1

    def h_copy(side, u):
        return pltpu.make_async_remote_copy(
            src_ref=h_out.at[side, u],
            dst_ref=h_in.at[1 - side, u],
            send_sem=h_ss.at[side, u],
            recv_sem=h_rs.at[1 - side, u],
            device_id=((left, right)[side], mm),
            device_id_type=MESH,
        )

    def d_copy(side):
        return pltpu.make_async_remote_copy(
            src_ref=d_out.at[side],
            dst_ref=d_in.at[1 - side],
            send_sem=d_ss.at[side],
            recv_sem=d_rs.at[1 - side],
            device_id=((left, right)[side], mm),
            device_id_type=MESH,
        )

    def y_copy(slot, to):
        return pltpu.make_async_remote_copy(
            src_ref=y_out.at[slot],
            dst_ref=t1.at[to, mine],
            send_sem=y_ss.at[slot],
            recv_sem=y_rs.at[slot],
            device_id=(mate, mm),
            device_id_type=MESH,
        )

    def m_copy(side, cg, h):
        start = 0 if side == 0 else band - REACH
        return pltpu.make_async_remote_copy(
            src_ref=t1.at[cg, h, :, pl.ds(start, REACH), :],
            dst_ref=m_in.at[1 - side, cg, h],
            send_sem=m_ss.at[side, cg, h],
            recv_sem=m_rs.at[1 - side, cg, h],
            device_id=(me, (up, down)[side]),
            device_id_type=MESH,
        )

    def m_start(cg, h):
        for side in range(2):
            @pl.when(has_map[side])
            def _(side=side):
                m_copy(side, cg, h).start()

    def dm_copy(side):
        return pltpu.make_async_remote_copy(
            src_ref=d_own,
            dst_ref=dm_in.at[1 - side],
            send_sem=dm_ss.at[side],
            recv_sem=dm_rs.at[1 - side],
            device_id=(me, (up, down)[side]),
            device_id_type=MESH,
        )

    for side in range(2):
        @pl.when(jnp.logical_not(has_map[side]))
        def _(side=side):
            dm_in[side] = jnp.zeros((cols, band), jnp.float32)
            m_in[side] = jnp.zeros(m_in.shape[1:], jnp.bfloat16)

    block = (UNIT, band, part)

    def rounded(u):
        at = pl.multiple_of(u * unit, unit)
        return acc[pl.ds(at, unit), :].astype(jnp.bfloat16).reshape(block)

    for side in range(2):
        take(final, (0, 1), (side,))
        for u in range(over_units):
            g = u if side == 0 else col_units + over_units + u
            contract(final, side, g, 1)
            h_out[side, u] = rounded(side * col_units + g)

            @pl.when(has_dp[side])
            def _(side=side, u=u):
                h_copy(side, u).start()

        if side == 0:
            def rest(i, none):
                contract(final, 0, (i + 1) * over_units, over_units)
                return none

            lax.fori_loop(0, span_units // over_units - 1, rest, 0)

    for m in range(spare):
        n = col_units + m - mine * spare
        contract(final, 1, n - spare, 1)
        y_out[m] = rounded(n + over_units)
        y_copy(m, m + mine * over_units).start()

    for m in range(spare):
        n = over_units + m + mine * spare
        contract(final, 1, n - spare, 1)
        t1[m + (1 - mine) * over_units, mine] = rounded(n + over_units)
        m_start(m + (1 - mine) * over_units, mine)

    ends = 2 * col_units - over_units
    for e in range(over_units):
        contract(final, 1, ends + e - spare, 1)
        if e >= spare:
            contract(final, 1, e - spare, 1)

    totals = []
    for tile in range(2):
        total = jnp.zeros((span, band), jnp.float32)
        for s in range(pairs):
            total += lax.dot_general(
                cw[tile, s].astype(jnp.bfloat16), rm[tile, s], NT, preferred_element_type=jnp.float32
            )
        totals.append(total)
    d_out[0] = totals[0][:REACH]
    d_out[1] = totals[1][REACH + cols :]
    d_own[...] = jnp.where(
        mine == 0, totals[0][REACH : REACH + cols], totals[1][REACH : REACH + cols]
    )
    d_own[pl.ds(pl.multiple_of((1 - mine) * (cols - REACH), 8), REACH), :] += jnp.where(
        mine == 0, totals[1][:REACH], totals[0][REACH + cols :]
    )
    for side in range(2):
        @pl.when(has_dp[side])
        def _(side=side):
            d_copy(side).start()

    for e in range(over_units):
        for side in range(2):
            @pl.when(has_dp[side])
            def _(side=side, e=e):
                h_copy(1 - side, e).wait_recv()
                at = (over_units + e if side == 0 else over_units + ends + e) * unit
                acc[pl.ds(at, unit), :] += h_in[side, e].reshape(unit, part).astype(jnp.float32)

        y_out[spare + e] = rounded(over_units + e + (1 - mine) * ends)
        y_copy(spare + e, e + (1 - mine) * spare).start()
        t1[e + mine * spare, mine] = rounded(over_units + e + mine * ends)
        m_start(e + mine * spare, mine)

    for side in range(2):
        @pl.when(has_dp[side])
        def _(side=side):
            d_copy(1 - side).wait_recv()

        @pl.when(has_dp[side] & (mine == side))
        def _(side=side):
            base = 0 if side == 0 else cols - REACH
            d_own[pl.ds(base, REACH), :] += d_in[side]

    for side in range(2):
        @pl.when(has_map[side])
        def _(side=side):
            dm_copy(side).start()

    gap = iota((band, band + 2 * REACH), 0) + REACH - iota((band, band + 2 * REACH), 1)
    taps = weight(gap.astype(jnp.float32)).astype(jnp.bfloat16)

    def finish(u, h):
        for side in range(2):
            @pl.when(has_map[side])
            def _(side=side):
                m_copy(1 - side, u, h).wait_recv()

        for i in range(0, UNIT, 2):
            ext = jnp.concatenate(
                [
                    jnp.concatenate([m_in[0, u, h, i + k], t1[u, h, i + k], m_in[1, u, h, i + k]], axis=0)
                    for k in range(2)
                ],
                axis=1,
            )
            got = jnp.dot(taps, ext, preferred_element_type=jnp.float32).astype(jnp.bfloat16)
            for k in range(2):
                num_ref[u * UNIT + i + k, :, pl.ds(pl.multiple_of(h * part, part), part)] = got[
                    :, k * part : (k + 1) * part
                ]

    for m in range(spare):
        y_copy(m, 0).wait_recv()
        m_start(m + (1 - mine) * over_units, 1 - mine)
    for m in range(spare):
        finish(m + (1 - mine) * over_units, mine)
    for side in range(2):
        @pl.when(has_map[side])
        def _(side=side):
            dm_copy(1 - side).wait_recv()

    den = jnp.zeros((cols, band), jnp.float32)
    apart = (iota((band, band), 0) - iota((band, band), 1)).astype(jnp.float32)
    for p, counts in enumerate((dm_in[0], d_own[...], dm_in[1])):
        row_taps = weight(apart + float((1 - p) * band)).astype(jnp.bfloat16).astype(jnp.float32)
        den += lax.dot_general(
            counts, row_taps, NT, precision=lax.Precision.HIGHEST, preferred_element_type=jnp.float32
        )
    scale_ref[...] = 0.9 / (den + 1.0)
    for e in range(over_units):
        finish(e + mine * spare, mine)
    for m in range(spare):
        finish(m + (1 - mine) * over_units, 1 - mine)
    for e in range(over_units):
        y_copy(spare + e, 0).wait_recv()
        m_start(e + mine * spare, 1 - mine)
    for e in range(over_units):
        finish(e + mine * spare, 1 - mine)

    def sent(i, none):
        s, tile = i // 2, i % 2
        for to in range(2):
            @pl.when((s < last) | (mine != to))
            def _(to=to):
                k_copy(s, tile, to, mine).wait_send()
                x_copy(s, tile, to, mine).wait_send()

        return none

    lax.fori_loop(0, 2 * pairs, sent, 0)
    for u in range(col_units):
        y_copy(u, 0).wait_send()
    for side in range(2):
        @pl.when(has_dp[side])
        def _(side=side):
            d_copy(side).wait_send()
            for u in range(over_units):
                h_copy(side, u).wait_send()

        @pl.when(has_map[side])
        def _(side=side):
            dm_copy(side).wait_send()
            for u in range(col_units):
                for h in range(HALVES):
                    m_copy(side, u, h).wait_send()


def on_device(embeddings, winners, codebook):
    cols, band, width = codebook.shape
    n_dp = lax.axis_size("dp")
    n_map = lax.axis_size("map")
    rows = embeddings.shape[0]
    cap = max(2, 2 * rows // (n_dp * n_map))
    slots = n_dp * cap
    part = width // HALVES
    pairs = n_dp // 2
    units = cols // UNIT
    past = REACH // UNIT
    unit = UNIT * band
    span = cols + 2 * REACH
    bf16, f32 = jnp.bfloat16, jnp.float32
    vmem = pl.BlockSpec(memory_space=pltpu.VMEM)
    dma = pltpu.SemaphoreType.DMA
    num, scale = pl.pallas_call(
        functools.partial(exchange_kernel, (n_dp, n_map, cap, cols, band, rows, width)),
        out_shape=(
            jax.ShapeDtypeStruct((cols, band, width), bf16),
            jax.ShapeDtypeStruct((cols, band), f32),
        ),
        in_specs=[pl.BlockSpec(memory_space=pl.ANY), vmem],
        out_specs=(vmem, vmem),
        scratch_shapes=[
            pltpu.VMEM((rows, width), bf16),
            pltpu.VMEM((n_dp, rows), f32),
            pltpu.VMEM((n_dp, cap), f32),
            pltpu.VMEM((pairs, HALVES, 2, cap, part), bf16),
            pltpu.VMEM((2, slots, part), bf16),
            pltpu.VMEM((pairs, 2, 8, cap), f32),
            pltpu.VMEM((pairs, 2, 2, 8, cap), f32),
            pltpu.VMEM((2, pairs, span, 2 * cap), f32),
            pltpu.VMEM((2, pairs, band, 2 * cap), bf16),
            pltpu.VMEM((2 * REACH * band, 2 * cap), bf16),
            pltpu.VMEM((2 * (units + past) * unit, part), f32),
            pltpu.VMEM((2, past, UNIT, band, part), bf16),
            pltpu.VMEM((2, past, UNIT, band, part), bf16),
            pltpu.VMEM((2, REACH, band), f32),
            pltpu.VMEM((2, REACH, band), f32),
            pltpu.VMEM((cols, band), f32),
            pltpu.VMEM((units, UNIT, band, part), bf16),
            pltpu.VMEM((units, HALVES, UNIT, band, part), bf16),
            pltpu.VMEM((2, units, HALVES, UNIT, REACH, part), bf16),
            pltpu.VMEM((2, cols, band), f32),
            dma,
            dma((pairs, 2, 2)), dma((pairs, 2, 2)), dma((pairs, 2, 2)), dma((pairs, 2, 2)),
            dma((2, past)), dma((2, past)), dma((2,)), dma((2,)), dma((units,)), dma((units,)),
            dma((2, units, HALVES)), dma((2, units, HALVES)), dma((2,)), dma((2,)),
        ],
        compiler_params=pltpu.CompilerParams(
            collective_id=0, has_side_effects=True, vmem_limit_bytes=56 * 1024 * 1024
        ),
        cost_estimate=pl.CostEstimate(
            flops=2 * width * slots * (rows + span * band),
            bytes_accessed=2 * width * (rows + cols * (band + 2 * REACH)),
            transcendentals=span * slots,
        ),
    )(embeddings, winners.reshape(1, rows))

    updated = 0.1 * codebook + (num.astype(f32) + codebook) * scale[:, :, None]
    return updated, updated.astype(bf16)


def solution(mesh):
    placed = (P("dp", None), P("dp"), P("dp", "map", None))
    return jax.shard_map(
        on_device,
        mesh=mesh,
        in_specs=placed,
        out_specs=(P("dp", "map", None), P("dp", "map", None)),
        check_vma=False,
    )
```

```python
import functools

import jax
import jax.numpy as jnp
from jax import lax
from jax.experimental import pallas as pl
from jax.experimental.pallas import tpu as pltpu
from jax.sharding import PartitionSpec as P

REACH = 16
SIGMA = float(REACH) / 2.0
HALVES = 2
UNIT = REACH // 2
MESH = pl.DeviceIdType.MESH
NT = (((1,), (1,)), ((), ()))


def iota(shape, dim):
    return lax.broadcasted_iota(jnp.int32, shape, dim)


def over(values, size):
    if size & (size - 1) == 0:
        return lax.shift_right_logical(values, jnp.int32(size.bit_length() - 1))
    return values // size


def weight(gap):
    apart = gap / SIGMA
    return jnp.where(jnp.abs(gap) <= REACH, jnp.exp(-0.5 * apart * apart) / SIGMA, 0.0)


def exchange_kernel(
    dims, emb_hbm, win_ref, num_ref, scale_ref,
    emb, rank, keys, x_out, x_in, k_out, k_in, cw, rm, mix, acc, h_out, h_in, d_out, d_in, d_own, y_out, t1, m_in,
    dm_in, e_sem, x_ss, x_rs, k_ss, k_rs, h_ss, h_rs, d_ss, d_rs, y_ss, y_rs, m_ss, m_rs, dm_ss, dm_rs,
):
    n_dp, n_map, cap, cols, band, rows, width = dims
    part = width // HALVES
    unit = UNIT * band
    over_units = REACH // UNIT
    col_units = cols // UNIT
    spare = col_units - over_units
    span_units = col_units + 2 * over_units
    pairs = n_dp // 2
    me = lax.axis_index("dp")
    mm = lax.axis_index("map")
    pair, mine = me // 2, me % 2
    mate = 2 * pair + 1 - mine
    left, right = lax.rem(me + n_dp - 2, n_dp), lax.rem(me + 2, n_dp)
    up, down = lax.rem(mm + n_map - 1, n_map), lax.rem(mm + 1, n_map)
    has_dp = (pair > 0, pair < pairs - 1)
    has_map = (mm > 0, mm < n_map - 1)

    fetch = pltpu.make_async_copy(emb_hbm, emb, e_sem)
    fetch.start()
    barrier = pltpu.get_barrier_semaphore()
    for k in range(1, n_dp):
        pl.semaphore_signal(
            barrier, inc=1, device_id=(lax.rem(me + k, n_dp), mm), device_id_type=MESH
        )
    for other in (up, down):
        pl.semaphore_signal(barrier, inc=1, device_id=(me, other), device_id_type=MESH)

    win = win_ref[...]
    column = over(win, band * n_map)
    row_of = win - column * (band * n_map) - mm * band
    target = over(column, cols)
    local = column - target * cols
    inside = (row_of >= 0) & (row_of < band)
    target = jnp.where(inside, target, -1)
    step = 256
    upper = jnp.where(iota((step, step), 0) <= iota((step, step), 1), 1.0, 0.0).astype(jnp.bfloat16)
    hits = jnp.where(target == iota((n_dp, rows), 0), 1.0, 0.0)
    carry = jnp.zeros((n_dp, 1), jnp.float32)
    for j in range(rows // step):
        hit = hits[:, j * step : (j + 1) * step]
        count = jnp.dot(hit.astype(jnp.bfloat16), upper, preferred_element_type=jnp.float32) + carry
        carry = count[:, step - 1 : step]
        rank[:, j * step : (j + 1) * step] = jnp.where(hit > 0.0, count - 1.0, -1.0)

    high = cap // 16
    slot = jnp.max(rank[...], axis=0, keepdims=True).astype(jnp.int32)
    where_high = jnp.where(slot >= 0, target * high + over(slot, 16), -1)
    tall = jnp.where(iota((n_dp * high, rows), 0) == where_high, 1.0, 0.0).astype(jnp.bfloat16)
    low = iota((16, rows), 0) == slot % 16
    tags = jnp.concatenate(
        [jnp.where(low, of.astype(jnp.float32), 0.0) for of in (local, row_of, jnp.ones_like(local))], axis=0
    ).astype(jnp.bfloat16)
    table = lax.dot_general(tall, tags, NT, preferred_element_type=jnp.float32)
    lane = iota((48, cap), 0)
    spread = jnp.where(
        lane % 16 == iota((48, cap), 1) % 16, jnp.where(lane < 16, float(band), 1.0), 0.0
    ).astype(jnp.bfloat16)
    table = jnp.dot(table.astype(jnp.bfloat16), spread, preferred_element_type=jnp.float32)
    table = jnp.where(iota((n_dp * high, cap), 0) % high == over(iota((n_dp * high, cap), 1), 16), table, 0.0)
    join = jnp.where(iota((n_dp, n_dp * high), 0) == over(iota((n_dp, n_dp * high), 1), high), 1.0, 0.0)
    keys[...] = jnp.dot(
        join, table, precision=lax.Precision.HIGHEST, preferred_element_type=jnp.float32
    )

    fetch.wait()
    pl.semaphore_wait(barrier, n_dp + 1)

    def plane(s):
        half = (s + 1) // 2
        return lax.rem(pair + pairs // 2 + half * (1 - 2 * (s % 2)), pairs)

    def place(s, sender):
        return pl.ds(pl.multiple_of((2 * s + sender) * cap, cap), cap)

    def x_copy(s, tile, to, sender):
        return pltpu.make_async_remote_copy(
            src_ref=x_out.at[s, to, tile],
            dst_ref=x_in.at[tile, place(s, sender), :],
            send_sem=x_ss.at[s, to, tile],
            recv_sem=x_rs.at[s, sender, tile],
            device_id=(2 * plane(s) + to, mm),
            device_id_type=MESH,
        )

    def k_copy(s, tile, to, sender):
        return pltpu.make_async_remote_copy(
            src_ref=k_out.at[s, tile],
            dst_ref=k_in.at[s, sender, tile],
            send_sem=k_ss.at[s, to, tile],
            recv_sem=k_rs.at[s, sender, tile],
            device_id=(2 * plane(s) + to, mm),
            device_id_type=MESH,
        )

    last = pairs - 1

    def send_keys(i, none):
        s, tile = i // 2, i % 2
        k_out[s, tile] = jnp.broadcast_to(keys[pl.ds(2 * plane(s) + tile, 1), :], (8, cap))

        @pl.when(s < last)
        def _():
            for to in range(2):
                k_copy(s, tile, to, mine).start()

        @pl.when(s == last)
        def _():
            k_copy(s, tile, 1 - mine, mine).start()
            k_in[s, mine, tile] = k_out[s, tile]

        return none

    lax.fori_loop(0, 2 * pairs, send_keys, 0)
    piece = rows // 4
    slot_of = iota((cap, piece), 0).astype(jnp.float32).astype(jnp.bfloat16)
    one, nought = jnp.bfloat16(1.0), jnp.bfloat16(0.0)

    def send(s, none):
        packed = jnp.zeros((2 * cap, width), jnp.float32)
        for q in range(4):
            chosen = jnp.concatenate(
                [
                    jnp.where(
                        rank[pl.ds(2 * plane(s) + tile, 1), q * piece : (q + 1) * piece].astype(jnp.bfloat16)
                        == slot_of,
                        one,
                        nought,
                    )
                    for tile in range(2)
                ],
                axis=0,
            )
            packed += jnp.dot(
                chosen, emb[q * piece : (q + 1) * piece, :], preferred_element_type=jnp.float32
            )
        packed = packed.astype(jnp.bfloat16)
        for tile in range(2):
            for h in range(HALVES):
                x_out[s, h, tile] = packed[tile * cap : (tile + 1) * cap, h * part : (h + 1) * part]

        @pl.when(s < last)
        def _():
            for tile in range(2):
                for to in range(2):
                    x_copy(s, tile, to, mine).start()

        @pl.when(s == last)
        def _():
            for tile in range(2):
                x_copy(s, tile, 1 - mine, mine).start()
                x_in[tile, place(s, mine), :] = x_out[s, mine, tile]

        return none

    lax.fori_loop(0, pairs, send, 0)
    acc[...] = jnp.zeros_like(acc)

    span = cols + 2 * REACH

    def take(s, senders):
        for sender in senders:
            for tile in range(2):
                k_copy(s, tile, 1 - mine, sender).wait_recv()
                x_copy(s, tile, 1 - mine, sender).wait_recv()
        for sender in range(2):
            for tile in range(2):
                key = k_in[s, sender, tile][0:1, :].astype(jnp.int32) - 1
                at = over(key, band)
                gap = (iota((span, cap), 0) - REACH - at).astype(jnp.float32)
                lanes = slice(sender * cap, (sender + 1) * cap)
                cw[tile, s, :, lanes] = weight(gap)
                rm[tile, s, :, lanes] = jnp.where(
                    iota((band, cap), 0) == key - at * band, 1.0, 0.0
                ).astype(jnp.bfloat16)

    def contract(s, tile, g, count):
        lines = rm[tile, s]
        for i in range(UNIT * count):
            line = jnp.broadcast_to(cw[tile, s, pl.ds(g * UNIT + i, 1), :], (band, 2 * cap))
            mix[i * band : (i + 1) * band, :] = line.astype(jnp.bfloat16) * lines
        at = pl.multiple_of((tile * col_units + g) * unit, unit)
        acc[pl.ds(at, unit * count), :] += jnp.dot(
            mix[pl.ds(0, unit * count), :],
            x_in[tile, pl.ds(pl.multiple_of(2 * s * cap, 2 * cap), 2 * cap), :],
            preferred_element_type=jnp.float32,
        )

    def add_step(s):
        count = span_units // over_units

        def one(i, none):
            contract(s, i // count, i % count * over_units, over_units)
            return none

        lax.fori_loop(0, 2 * count, one, 0)

    def middle_steps(s, none):
        take(s, (0, 1))
        add_step(s)
        return none

    lax.fori_loop(0, last, middle_steps, 0)
    final = last
    take(final, (1 - mine,))

    def h_copy(side, u):
        return pltpu.make_async_remote_copy(
            src_ref=h_out.at[side, u],
            dst_ref=h_in.at[1 - side, u],
            send_sem=h_ss.at[side, u],
            recv_sem=h_rs.at[1 - side, u],
            device_id=((left, right)[side], mm),
            device_id_type=MESH,
        )

    def d_copy(side):
        return pltpu.make_async_remote_copy(
            src_ref=d_out.at[side],
            dst_ref=d_in.at[1 - side],
            send_sem=d_ss.at[side],
            recv_sem=d_rs.at[1 - side],
            device_id=((left, right)[side], mm),
            device_id_type=MESH,
        )

    def y_copy(slot, to):
        return pltpu.make_async_remote_copy(
            src_ref=y_out.at[slot],
            dst_ref=t1.at[to, mine],
            send_sem=y_ss.at[slot],
            recv_sem=y_rs.at[slot],
            device_id=(mate, mm),
            device_id_type=MESH,
        )

    def m_copy(side, cg, h):
        start = 0 if side == 0 else band - REACH
        return pltpu.make_async_remote_copy(
            src_ref=t1.at[cg, h, :, pl.ds(start, REACH), :],
            dst_ref=m_in.at[1 - side, cg, h],
            send_sem=m_ss.at[side, cg, h],
            recv_sem=m_rs.at[1 - side, cg, h],
            device_id=(me, (up, down)[side]),
            device_id_type=MESH,
        )

    def m_start(cg, h):
        for side in range(2):
            @pl.when(has_map[side])
            def _(side=side):
                m_copy(side, cg, h).start()

    def dm_copy(side):
        return pltpu.make_async_remote_copy(
            src_ref=d_own,
            dst_ref=dm_in.at[1 - side],
            send_sem=dm_ss.at[side],
            recv_sem=dm_rs.at[1 - side],
            device_id=(me, (up, down)[side]),
            device_id_type=MESH,
        )

    for side in range(2):
        @pl.when(jnp.logical_not(has_map[side]))
        def _(side=side):
            dm_in[side] = jnp.zeros((cols, band), jnp.float32)
            m_in[side] = jnp.zeros(m_in.shape[1:], jnp.bfloat16)

    block = (UNIT, band, part)

    def rounded(u):
        at = pl.multiple_of(u * unit, unit)
        return acc[pl.ds(at, unit), :].astype(jnp.bfloat16).reshape(block)

    for u in range(over_units):
        for side in range(2):
            g = u if side == 0 else col_units + over_units + u
            contract(final, side, g, 1)
            h_out[side, u] = rounded(side * col_units + g)

            @pl.when(has_dp[side])
            def _(side=side, u=u):
                h_copy(side, u).start()

    for m in range(spare):
        n = col_units + m - mine * spare
        contract(final, 0, n + over_units, 1)
        contract(final, 1, n - spare, 1)
        y_out[m] = rounded(n + over_units)
        y_copy(m, m + mine * over_units).start()

    for m in range(spare):
        n = over_units + m + mine * spare
        contract(final, 0, n + over_units, 1)
        contract(final, 1, n - spare, 1)
        t1[m + (1 - mine) * over_units, mine] = rounded(n + over_units)
        m_start(m + (1 - mine) * over_units, mine)

    ends = 2 * col_units - over_units
    for e in range(over_units):
        contract(final, 0, e + over_units, 1)
        contract(final, 1, ends + e - spare, 1)
        if e >= spare:
            contract(final, 1, e - spare, 1)
            contract(final, 0, ends + e + over_units, 1)

    totals = []
    for tile in range(2):
        total = jnp.zeros((span, band), jnp.float32)
        for s in range(pairs):
            total += lax.dot_general(
                cw[tile, s].astype(jnp.bfloat16), rm[tile, s], NT, preferred_element_type=jnp.float32
            )
        totals.append(total)
    d_out[0] = totals[0][:REACH]
    d_out[1] = totals[1][REACH + cols :]
    d_own[...] = jnp.where(
        mine == 0, totals[0][REACH : REACH + cols], totals[1][REACH : REACH + cols]
    )
    d_own[pl.ds(pl.multiple_of((1 - mine) * (cols - REACH), 8), REACH), :] += jnp.where(
        mine == 0, totals[1][:REACH], totals[0][REACH + cols :]
    )
    for side in range(2):
        @pl.when(has_dp[side])
        def _(side=side):
            d_copy(side).start()

    for e in range(over_units):
        for side in range(2):
            @pl.when(has_dp[side])
            def _(side=side, e=e):
                h_copy(1 - side, e).wait_recv()
                at = (over_units + e if side == 0 else over_units + ends + e) * unit
                acc[pl.ds(at, unit), :] += h_in[side, e].reshape(unit, part).astype(jnp.float32)

        y_out[spare + e] = rounded(over_units + e + (1 - mine) * ends)
        y_copy(spare + e, e + (1 - mine) * spare).start()
        t1[e + mine * spare, mine] = rounded(over_units + e + mine * ends)
        m_start(e + mine * spare, mine)

    for side in range(2):
        @pl.when(has_dp[side])
        def _(side=side):
            d_copy(1 - side).wait_recv()

        @pl.when(has_dp[side] & (mine == side))
        def _(side=side):
            base = 0 if side == 0 else cols - REACH
            d_own[pl.ds(base, REACH), :] += d_in[side]

    for side in range(2):
        @pl.when(has_map[side])
        def _(side=side):
            dm_copy(side).start()

    gap = iota((band, band + 2 * REACH), 0) + REACH - iota((band, band + 2 * REACH), 1)
    taps = weight(gap.astype(jnp.float32)).astype(jnp.bfloat16)

    def finish(u, h):
        for side in range(2):
            @pl.when(has_map[side])
            def _(side=side):
                m_copy(1 - side, u, h).wait_recv()

        for i in range(0, UNIT, 2):
            ext = jnp.concatenate(
                [
                    jnp.concatenate([m_in[0, u, h, i + k], t1[u, h, i + k], m_in[1, u, h, i + k]], axis=0)
                    for k in range(2)
                ],
                axis=1,
            )
            got = jnp.dot(taps, ext, preferred_element_type=jnp.float32).astype(jnp.bfloat16)
            for k in range(2):
                num_ref[u * UNIT + i + k, :, pl.ds(pl.multiple_of(h * part, part), part)] = got[
                    :, k * part : (k + 1) * part
                ]

    for m in range(spare):
        y_copy(m, 0).wait_recv()
        m_start(m + (1 - mine) * over_units, 1 - mine)
    for m in range(spare):
        finish(m + (1 - mine) * over_units, mine)
    for side in range(2):
        @pl.when(has_map[side])
        def _(side=side):
            dm_copy(1 - side).wait_recv()

    den = jnp.zeros((cols, band), jnp.float32)
    apart = (iota((band, band), 0) - iota((band, band), 1)).astype(jnp.float32)
    for p, counts in enumerate((dm_in[0], d_own[...], dm_in[1])):
        row_taps = weight(apart + float((1 - p) * band)).astype(jnp.bfloat16).astype(jnp.float32)
        den += lax.dot_general(
            counts, row_taps, NT, precision=lax.Precision.HIGHEST, preferred_element_type=jnp.float32
        )
    scale_ref[...] = 0.9 / (den + 1.0)
    for e in range(over_units):
        finish(e + mine * spare, mine)
    for m in range(spare):
        finish(m + (1 - mine) * over_units, 1 - mine)
    for e in range(over_units):
        y_copy(spare + e, 0).wait_recv()
        m_start(e + mine * spare, 1 - mine)
    for e in range(over_units):
        finish(e + mine * spare, 1 - mine)

    def sent(i, none):
        s, tile = i // 2, i % 2
        for to in range(2):
            @pl.when((s < last) | (mine != to))
            def _(to=to):
                k_copy(s, tile, to, mine).wait_send()
                x_copy(s, tile, to, mine).wait_send()

        return none

    lax.fori_loop(0, 2 * pairs, sent, 0)
    for u in range(col_units):
        y_copy(u, 0).wait_send()
    for side in range(2):
        @pl.when(has_dp[side])
        def _(side=side):
            d_copy(side).wait_send()
            for u in range(over_units):
                h_copy(side, u).wait_send()

        @pl.when(has_map[side])
        def _(side=side):
            dm_copy(side).wait_send()
            for u in range(col_units):
                for h in range(HALVES):
                    m_copy(side, u, h).wait_send()


def on_device(embeddings, winners, codebook):
    cols, band, width = codebook.shape
    n_dp = lax.axis_size("dp")
    n_map = lax.axis_size("map")
    rows = embeddings.shape[0]
    cap = max(2, 2 * rows // (n_dp * n_map))
    slots = n_dp * cap
    part = width // HALVES
    pairs = n_dp // 2
    units = cols // UNIT
    past = REACH // UNIT
    unit = UNIT * band
    span = cols + 2 * REACH
    bf16, f32 = jnp.bfloat16, jnp.float32
    vmem = pl.BlockSpec(memory_space=pltpu.VMEM)
    dma = pltpu.SemaphoreType.DMA
    num, scale = pl.pallas_call(
        functools.partial(exchange_kernel, (n_dp, n_map, cap, cols, band, rows, width)),
        out_shape=(
            jax.ShapeDtypeStruct((cols, band, width), bf16),
            jax.ShapeDtypeStruct((cols, band), f32),
        ),
        in_specs=[pl.BlockSpec(memory_space=pl.ANY), vmem],
        out_specs=(vmem, vmem),
        scratch_shapes=[
            pltpu.VMEM((rows, width), bf16),
            pltpu.VMEM((n_dp, rows), f32),
            pltpu.VMEM((n_dp, cap), f32),
            pltpu.VMEM((pairs, HALVES, 2, cap, part), bf16),
            pltpu.VMEM((2, slots, part), bf16),
            pltpu.VMEM((pairs, 2, 8, cap), f32),
            pltpu.VMEM((pairs, 2, 2, 8, cap), f32),
            pltpu.VMEM((2, pairs, span, 2 * cap), f32),
            pltpu.VMEM((2, pairs, band, 2 * cap), bf16),
            pltpu.VMEM((REACH * band, 2 * cap), bf16),
            pltpu.VMEM((2 * (units + past) * unit, part), f32),
            pltpu.VMEM((2, past, UNIT, band, part), bf16),
            pltpu.VMEM((2, past, UNIT, band, part), bf16),
            pltpu.VMEM((2, REACH, band), f32),
            pltpu.VMEM((2, REACH, band), f32),
            pltpu.VMEM((cols, band), f32),
            pltpu.VMEM((units, UNIT, band, part), bf16),
            pltpu.VMEM((units, HALVES, UNIT, band, part), bf16),
            pltpu.VMEM((2, units, HALVES, UNIT, REACH, part), bf16),
            pltpu.VMEM((2, cols, band), f32),
            dma,
            dma((pairs, 2, 2)), dma((pairs, 2, 2)), dma((pairs, 2, 2)), dma((pairs, 2, 2)),
            dma((2, past)), dma((2, past)), dma((2,)), dma((2,)), dma((units,)), dma((units,)),
            dma((2, units, HALVES)), dma((2, units, HALVES)), dma((2,)), dma((2,)),
        ],
        compiler_params=pltpu.CompilerParams(
            collective_id=0, has_side_effects=True, vmem_limit_bytes=56 * 1024 * 1024
        ),
        cost_estimate=pl.CostEstimate(
            flops=2 * width * slots * (rows + span * band),
            bytes_accessed=2 * width * (rows + cols * (band + 2 * REACH)),
            transcendentals=span * slots,
        ),
    )(embeddings, winners.reshape(1, rows))

    updated = 0.1 * codebook + (num.astype(f32) + codebook) * scale[:, :, None]
    return updated, updated.astype(bf16)


def solution(mesh):
    placed = (P("dp", None), P("dp"), P("dp", "map", None))
    return jax.shard_map(
        on_device,
        mesh=mesh,
        in_specs=placed,
        out_specs=(P("dp", "map", None), P("dp", "map", None)),
        check_vma=False,
    )
```
